32 devices in a mesh: outer: 8 (over y, x, core), inner: 4 (over z).
Axes of the slice: x: 2, y: 2, z: 4, core: 2. Of those that a mesh axis runs over, the one named last changes fastest.
Arguments:
- queries: bfloat16 [4096, 2048], P(('outer', 'inner')), may hold values from -6 to 6
- keys: bfloat16 [4096, 2, 2048], P(('outer', 'inner')), may hold values from -6 to 6
- values: bfloat16 [4096, 2, 2048], P(('outer', 'inner')), may hold values from -6 to 6
- beta_logit: float32 [2, 16, 4096], P(None, None, ('outer', 'inner')), may hold values from -1.5 to 11
- gain: float32 [2048], replicated, may hold values from 0.5 to 1.5
Outputs:
- mixed: bfloat16 [4096, 2048], P(('outer', 'inner'))
The draws below stay inside these ranges and needn't reach their ends.
All inputs are finite; a program needn't handle non-finite values.
Results may differ from the reference program's by a relative error of at most 0.0045.
Values sent between devices are 32-bit elements; how exact they have to be, the bound alone decides.
A program may use at most 64 MiB of HBM per device.

```python
import jax
import jax.numpy as jnp
from jax import lax

HEAD_COUNT = 16
HEAD = 128
TOK_DEV = 128
D = 2048
SEQUENCE_TOKENS = 4096


def draw_beta_logit(key, part):
    key = jax.random.fold_in(key, 7)
    key_collection = jax.random.split(key, 7)
    fast_count = HEAD_COUNT // 2
    slow_lo = 8.8
    order = jax.random.permutation(key_collection[0], HEAD_COUNT)
    fast = (order < fast_count)[None, :, None]
    blocks = SEQUENCE_TOKENS // TOK_DEV
    base = jax.random.uniform(key_collection[1], (1, HEAD_COUNT, 1), jnp.float32, slow_lo, slow_lo + 1.0)
    block_shift = jax.random.uniform(key_collection[2], (1, HEAD_COUNT, blocks), jnp.float32, -0.5, 0.5)
    block_shift = jnp.repeat(block_shift, TOK_DEV, axis=2)
    noise = jax.random.uniform(key_collection[3], (2, HEAD_COUNT, SEQUENCE_TOKENS), jnp.float32, -0.5, 0.5)
    gradual_segment = base + block_shift + noise
    quick = jax.random.uniform(key_collection[4], (2, HEAD_COUNT, SEQUENCE_TOKENS), jnp.float32, -1.5, 1.5)
    starts = jax.random.randint(key_collection[5], (HEAD_COUNT, 3), 0, SEQUENCE_TOKENS - 32)
    positions = jnp.arange(SEQUENCE_TOKENS, dtype=jnp.int32)[None, None, :]
    interior_part = (positions >= starts[:, :, None]) & (positions < starts[:, :, None] + 32)
    rapid_segment = jnp.any(interior_part, axis=1)[None]
    rapid_segment_values = jax.random.uniform(key_collection[6], (2, HEAD_COUNT, SEQUENCE_TOKENS), jnp.float32, -0.5, 0.5)
    gradual_segment = jnp.where(rapid_segment, rapid_segment_values, gradual_segment)
    return jnp.clip(jnp.where(fast, quick, gradual_segment), -1.5, 11.0).astype(jnp.float32)


def level_of(stream_key, extent, cuts, least, largest):
    level, own = 1.0, jax.random.fold_in(stream_key, 6)
    for axis_at, blocks in cuts:
        draws = jnp.exp(jax.random.uniform(jax.random.fold_in(own, axis_at), (blocks,), jnp.float32, least / len(cuts), largest / len(cuts)))
        level = level * jnp.repeat(draws, extent[axis_at] // blocks).reshape([-1 if axis == axis_at else 1 for axis in range(len(extent))])
    return level


def normal_values(stream_key, dims, spread, bound, cuts=(), kind=jnp.bfloat16):
    values = jax.random.normal(stream_key, dims, jnp.float32) * spread
    if len(cuts) > 0:
        values = level_of(stream_key, dims, cuts, -0.22, 0.18) * values
    return jnp.clip(values, min=-bound, max=bound).astype(kind)


def setup_inputs(seed: int = 0) -> dict:
    seeds = jax.random.split(jax.random.key(seed), 6)
    return {
        "queries": normal_values(seeds[0], (SEQUENCE_TOKENS, D), 1.0, 6.0, ((0, 32),)),
        "keys": normal_values(seeds[1], (SEQUENCE_TOKENS, 2, D), 1.0, 6.0, ((0, 32),)),
        "values": normal_values(seeds[2], (SEQUENCE_TOKENS, 2, D), 1.0, 6.0, ((0, 32),)),
        "beta_logit": draw_beta_logit(jax.random.fold_in(seeds[5], 71), 0),
        "gain": jnp.clip(1.0 + 0.1 * jax.random.normal(seeds[4], (D,), jnp.float32), 0.5, 1.5),
    }


HIGH = lax.Precision.HIGHEST

def unit_rows(field):
    return field / jnp.sqrt(lax.optimization_barrier(jnp.sum(field * field, axis=-1, keepdims=True)) + 1e-06)

def block_terms(queries, keys, values, logits):
    count = queries.shape[0]
    heads = logits.shape[1]
    size = queries.shape[1] // heads
    rows = 2 * count
    qf = unit_rows(queries.astype(jnp.float32).reshape(count, heads, size).transpose(1, 0, 2))
    kf = unit_rows(keys.astype(jnp.float32).reshape(count, 2, heads, size).transpose(2, 0, 1, 3).reshape(heads, rows, size))
    vf = values.astype(jnp.float32).reshape(count, 2, heads, size).transpose(2, 0, 1, 3).reshape(heads, rows, size)
    beta = (2.0 * jax.nn.sigmoid(logits)).transpose(1, 2, 0).reshape(heads, rows)
    gram = jnp.einsum('hrd,hsd->hrs', kf, kf, precision=HIGH)
    row_ids = lax.broadcasted_iota(jnp.int32, (rows, rows), 0)
    col_ids = lax.broadcasted_iota(jnp.int32, (rows, rows), 1)
    strict = (row_ids > col_ids)[None]
    eye_rows = jnp.eye(rows, dtype=jnp.float32)[None]
    system = eye_rows + jnp.where(strict, gram * beta[:, None, :], 0.0)
    both = jnp.concatenate([vf, kf], axis=-1)
    solved = lax.linalg.triangular_solve(system, both, left_side=True, lower=True, unit_diagonal=True)
    fresh = solved[..., :size]
    wmat = solved[..., size:]
    kscaled = kf * beta[:, :, None]
    trans = jnp.eye(size, dtype=jnp.float32)[None] - jnp.einsum('hrd,hre->hde', kscaled, wmat, precision=HIGH)
    offset = jnp.einsum('hrd,hre->hde', kscaled, fresh, precision=HIGH)
    scores = jnp.einsum('htd,hsd->hts', qf, kscaled, precision=HIGH)
    tok_ids = lax.broadcasted_iota(jnp.int32, (count, rows), 0)
    virt_ids = lax.broadcasted_iota(jnp.int32, (count, rows), 1)
    scores = jnp.where((virt_ids <= 2 * tok_ids + 1)[None], scores, 0.0)
    local_out = jnp.einsum('hts,hse->hte', scores, fresh, precision=HIGH)
    carried_q = qf - jnp.einsum('hts,hsd->htd', scores, wmat, precision=HIGH)
    return (trans, offset, local_out, carried_q)

def finish(local_out, carried_q, state, gain):
    heads, count, size = local_out.shape
    outs = local_out + jnp.einsum('htd,hde->hte', carried_q, state, precision=HIGH)
    scale = jnp.sqrt(lax.optimization_barrier(jnp.mean(outs * outs, axis=-1, keepdims=True)) + 1e-06)
    normed = outs / scale * gain.reshape(heads, 1, size)
    return normed.transpose(1, 0, 2).reshape(count, heads * size).astype(jnp.bfloat16)

def reference(queries, keys, values, beta_logit, gain):
    blocks = SEQUENCE_TOKENS // TOK_DEV
    q_blocks = queries.reshape(blocks, TOK_DEV, D)
    k_blocks = keys.reshape(blocks, TOK_DEV, 2, D)
    v_blocks = values.reshape(blocks, TOK_DEV, 2, D)
    l_blocks = beta_logit.reshape(2, HEAD_COUNT, blocks, TOK_DEV).transpose(2, 0, 1, 3)

    def advance(state, pieces):
        q_blk, k_blk, v_blk, l_blk = pieces
        trans, offset, local_out, carried_q = block_terms(q_blk, k_blk, v_blk, l_blk)
        result = finish(local_out, carried_q, state, gain)
        state = jnp.einsum('hde,hef->hdf', trans, state, precision=HIGH) + offset
        return (state, result)
    start = jnp.zeros((HEAD_COUNT, HEAD, HEAD), jnp.float32)
    _, mixed = lax.scan(advance, start, (q_blocks, k_blocks, v_blocks, l_blocks))
    return mixed.reshape(SEQUENCE_TOKENS, D)
```

```python
import functools

import jax
import jax.numpy as jnp
from jax import lax
from jax.experimental import pallas as pl
from jax.experimental.pallas import tpu as pltpu
from jax.sharding import PartitionSpec as P

F32 = jnp.float32
BF16 = jnp.bfloat16
MESH = pl.DeviceIdType.MESH
GROUP = 4


def dot(a, b):
    return lax.dot_general(a, b, (((1,), (0,)), ((), ())), preferred_element_type=F32)


def dot_nt(a, b):
    return lax.dot_general(a, b, (((1,), (1,)), ((), ())), preferred_element_type=F32)


def dot_tn(a, b):
    return lax.dot_general(a, b, (((0,), (0,)), ((), ())), preferred_element_type=F32)


def split(x):
    hi = x.astype(BF16)
    return hi, (x - hi.astype(F32)).astype(BF16)


def dot3(a, b):
    ah, al = split(a)
    bh, bl = split(b)
    return dot(ah, bh) + (dot(ah, bl) + dot(al, bh))


def unit_lower_inverses(systems, masks):
    size = systems[0].shape[0]
    eye = masks[0]
    out = [eye - n * masks[1] for n in systems]
    levels = size.bit_length() - 2
    for level in range(levels):
        mask = masks[2 + level]
        mid = [dot(n * mask, t).astype(BF16) for n, t in zip(systems, out)]
        out = [t - dot(t, m).astype(BF16) for t, m in zip(out, mid)]
    return out


def level_masks(size):
    row = lax.broadcasted_iota(jnp.int32, (size, size), 0)
    col = lax.broadcasted_iota(jnp.int32, (size, size), 1)
    lower = row > col
    masks = [(row == col)]
    for level in range(size.bit_length() - 1):
        same = (row >> (level + 1)) == (col >> (level + 1))
        apart = (row >> level) != (col >> level)
        masks.append(lower & same & apart)
    return [m.astype(F32).astype(BF16) for m in masks]


def local_kernel(q_ref, k_ref, v_ref, b_ref, maps_ref, outs_ref, mask_ref):
    count = q_ref.shape[0]
    rows = k_ref.shape[0]
    size = maps_ref.shape[1]
    half = rows // 2
    n_heads = maps_ref.shape[0]

    @pl.when(pl.program_id(0) == 0)
    def _():
        for at, m in enumerate(level_masks(half)):
            mask_ref[at] = m

    masks = [mask_ref[at] for at in range(mask_ref.shape[0])]
    row_h = lax.broadcasted_iota(jnp.int32, (half, half), 0)
    col_h = lax.broadcasted_iota(jnp.int32, (half, half), 1)
    strict = row_h > col_h
    beta_all = 2.0 / (1.0 + jnp.exp(-b_ref[0]))
    heads = range(n_heads)
    cols = [slice(h * size, (h + 1) * size) for h in heads]
    k = [k_ref[:, c] for c in cols]
    n00, n10, n11, rhs = [], [], [], []
    for h in heads:
        kf = k[h].astype(F32)
        inv = 1.0 / (jnp.sum(kf * kf, axis=-1, keepdims=True) + 1e-06)
        beta = beta_all[:, h : h + 1]
        coef = beta * inv
        k0, k1 = k[h][:half], k[h][half:]
        n00.append(split(jnp.where(strict, coef[:half] * dot_nt(k0, k0), 0.0)))
        n11.append(split(jnp.where(strict, coef[half:] * dot_nt(k1, k1), 0.0)))
        n10.append(split(coef[half:] * dot_nt(k1, k0)))
        vf = v_ref[:, cols[h]].astype(F32) * (beta * jnp.sqrt(inv))
        rhs.append(jnp.concatenate([vf, kf * coef], axis=1))
    inverse = unit_lower_inverses([n[0] for n in n00] + [n[0] for n in n11], masks)

    def solve(t, n, r):
        zh = dot(t, r.astype(BF16)).astype(BF16)
        res = (r - zh.astype(F32)) - (dot(n[0], zh) + dot(n[1], zh))
        return zh, dot(t, res.astype(BF16)).astype(BF16)

    top = [solve(inverse[h], n00[h], rhs[h][:half]) for h in heads]
    low = []
    for h in heads:
        th, tl = top[h]
        r = rhs[h][half:] - (dot(n10[h][0], th) + (dot(n10[h][1], th) + dot(n10[h][0], tl)))
        low.append(solve(inverse[n_heads + h], n11[h], r))
    eye = (row_h == col_h).astype(F32)
    tok = lax.broadcasted_iota(jnp.int32, (count, rows), 0)
    virt = lax.broadcasted_iota(jnp.int32, (count, rows), 1)
    seen = virt <= 2 * tok + 1
    for h in heads:
        zh = jnp.concatenate([top[h][0], low[h][0]], axis=0)
        zl = jnp.concatenate([top[h][1], low[h][1]], axis=0)
        kz = dot_tn(k[h], zh) + dot_tn(k[h], zl)
        maps_ref[h, :, :size] = eye - kz[:, size:]
        maps_ref[h, :, size:] = kz[:, :size]
        q = q_ref[:, cols[h]]
        qf = q.astype(F32)
        rq = lax.rsqrt(jnp.sum(qf * qf, axis=-1, keepdims=True) + 1e-06)
        ph, plo = split(jnp.where(seen, dot_nt(q, k[h]), 0.0))
        pz = dot(ph, zh) + (dot(plo, zh) + dot(ph, zl))
        outs_ref[h, :, :size] = pz[:, :size] * rq
        outs_ref[h, :, size:] = (qf - pz[:, size:]) * rq


def local_terms(queries, keys, values, logits):
    count, width = queries.shape
    heads = logits.shape[1]
    size = width // heads
    rows = 2 * count
    group = GROUP
    steps = heads // group
    half = rows // 2
    k2 = keys.reshape(rows, width)
    v2 = values.reshape(rows, width)
    b2 = logits.transpose(1, 2, 0).reshape(steps, group, rows).transpose(0, 2, 1)
    span = group * size
    return pl.pallas_call(
        local_kernel,
        grid=(steps,),
        in_specs=[
            pl.BlockSpec((count, span), lambda s: (0, s)),
            pl.BlockSpec((rows, span), lambda s: (0, s)),
            pl.BlockSpec((rows, span), lambda s: (0, s)),
            pl.BlockSpec((1, rows, group), lambda s: (s, 0, 0)),
        ],
        out_specs=[
            pl.BlockSpec((group, size, 2 * size), lambda s: (s, 0, 0)),
            pl.BlockSpec((group, count, 2 * size), lambda s: (s, 0, 0)),
        ],
        out_shape=[
            jax.ShapeDtypeStruct((heads, size, 2 * size), F32),
            jax.ShapeDtypeStruct((heads, count, 2 * size), F32),
        ],
        scratch_shapes=[pltpu.VMEM((half.bit_length(), half, half), BF16)],
        compiler_params=pltpu.CompilerParams(vmem_limit_bytes=48 * 1024 * 1024),
    )(queries, k2, v2, b2)


def chain_kernel(
    n_in, n_out, maps_ref, outs_ref, gain_ref, mixed_ref,
    comp, pre, state, after, s_pre, r_pre, s_chain, s_relay, r_state,
):
    heads, size = maps_ref.shape[0], maps_ref.shape[1]
    at, grp = lax.axis_index("inner"), lax.axis_index("outer")
    first, last = at == 0, at == n_in - 1
    has_prev = last & (grp > 0)
    has_next = last & (grp < n_out - 1)

    barrier = pltpu.get_barrier_semaphore()

    def greet(cond, dev):
        @pl.when(cond)
        def _():
            pl.semaphore_signal(barrier, inc=1, device_id=dev, device_id_type=MESH)

    greet(at > 0, (grp, at - 1))
    greet(at < n_in - 1, (grp, at + 1))
    greet(has_prev, (grp - 1, at))
    greet(has_next, (grp + 1, at))
    peers = sum(c.astype(jnp.int32) for c in (at > 0, at < n_in - 1, has_prev, has_next))
    pl.semaphore_wait(barrier, peers)

    def send_pre(h):
        return pltpu.make_async_remote_copy(
            comp.at[h], pre.at[h], s_pre.at[h], r_pre.at[h],
            device_id=(grp, at + 1), device_id_type=MESH)

    def send_chain(h):
        return pltpu.make_async_remote_copy(
            after.at[h], state.at[h], s_chain.at[h], r_state.at[h],
            device_id=(grp + 1, at), device_id_type=MESH)

    def send_relay(h):
        return pltpu.make_async_remote_copy(
            state.at[h], state.at[h], s_relay.at[h], r_state.at[h],
            device_id=(grp, at - 1), device_id_type=MESH)

    def prefix(h, _):
        @pl.when(first)
        def _():
            comp[h] = maps_ref[h]

        @pl.when(jnp.logical_not(first))
        def _():
            send_pre(h).wait_recv()
            own = maps_ref[h]
            both = dot3(own[:, :size], pre[h])
            comp[h, :, :size] = both[:, :size]
            comp[h, :, size:] = both[:, size:] + own[:, size:]

        @pl.when(jnp.logical_not(last))
        def _():
            send_pre(h).start()

        return 0

    lax.fori_loop(0, heads, prefix, 0)

    def finish(h, _):
        @pl.when(jnp.logical_not(last) | (grp > 0))
        def _():
            send_chain(h).wait_recv()

        @pl.when(last & (grp == 0))
        def _():
            state[h] = jnp.zeros((size, size), F32)

        @pl.when(has_next)
        def _():
            after[h] = dot3(comp[h, :, :size], state[h]) + comp[h, :, size:]
            send_chain(h).start()

        @pl.when(at > 0)
        def _():
            send_relay(h).start()

        def emit(entry):
            outs = outs_ref[h, :, :size] + dot3(outs_ref[h, :, size:], entry)
            scale = lax.rsqrt(jnp.mean(outs * outs, axis=-1, keepdims=True) + 1e-06)
            where = pl.ds(pl.multiple_of(h * size, size), size)
            mixed_ref[:, where] = (outs * scale * gain_ref[:, where]).astype(BF16)

        @pl.when(first)
        def _():
            emit(state[h])

        @pl.when(jnp.logical_not(first))
        def _():
            emit(dot3(pre[h, :, :size], state[h]) + pre[h, :, size:])

        return 0

    lax.fori_loop(0, heads, finish, 0)

    def drain(h, _):
        @pl.when(jnp.logical_not(last))
        def _():
            send_pre(h).wait_send()

        @pl.when(has_next)
        def _():
            send_chain(h).wait_send()

        @pl.when(at > 0)
        def _():
            send_relay(h).wait_send()

        return 0

    lax.fori_loop(0, heads, drain, 0)


def chained(maps, outs, gain):
    heads, size, _ = maps.shape
    count = outs.shape[1]
    n_in, n_out = lax.axis_size("inner"), lax.axis_size("outer")
    vmem = pl.BlockSpec(memory_space=pltpu.VMEM)
    sems = pltpu.SemaphoreType.DMA((heads,))
    return pl.pallas_call(
        functools.partial(chain_kernel, n_in, n_out),
        out_shape=jax.ShapeDtypeStruct((count, heads * size), BF16),
        in_specs=[vmem] * 3,
        out_specs=vmem,
        scratch_shapes=[
            pltpu.VMEM((heads, size, 2 * size), F32),
            pltpu.VMEM((heads, size, 2 * size), F32),
            pltpu.VMEM((heads, size, size), F32),
            pltpu.VMEM((heads, size, size), F32),
            sems, sems, sems, sems, sems,
        ],
        compiler_params=pltpu.CompilerParams(
            collective_id=0, has_side_effects=True, vmem_limit_bytes=48 * 1024 * 1024
        ),
    )(maps, outs, gain.reshape(1, -1))


def local(queries, keys, values, beta_logit, gain):
    maps, outs = local_terms(queries, keys, values, beta_logit)
    return chained(maps, outs, gain)


def solution(mesh):
    return jax.shard_map(
        local,
        mesh=mesh,
        in_specs=(
            P(("outer", "inner"), None),
            P(("outer", "inner"), None, None),
            P(("outer", "inner"), None, None),
            P(None, None, ("outer", "inner")),
            P(),
        ),
        out_specs=P(("outer", "inner"), None),
        check_vma=False,
    )
```

```python
import functools

import jax
import jax.numpy as jnp
from jax import lax
from jax.experimental import pallas as pl
from jax.experimental.pallas import tpu as pltpu
from jax.sharding import PartitionSpec as P

F32 = jnp.float32
BF16 = jnp.bfloat16
MESH = pl.DeviceIdType.MESH
GROUP = 4


def dot(a, b):
    return lax.dot_general(a, b, (((1,), (0,)), ((), ())), preferred_element_type=F32)


def dot_nt(a, b):
    return lax.dot_general(a, b, (((1,), (1,)), ((), ())), preferred_element_type=F32)


def dot_tn(a, b):
    return lax.dot_general(a, b, (((0,), (0,)), ((), ())), preferred_element_type=F32)


def split(x):
    hi = x.astype(BF16)
    return hi, (x - hi.astype(F32)).astype(BF16)


def dot3(a, b):
    ah, al = split(a)
    bh, bl = split(b)
    return dot(ah, bh) + (dot(ah, bl) + dot(al, bh))


def unit_lower_inverses(systems, masks):
    size = systems[0].shape[0]
    eye = masks[0]
    out = [eye - n * masks[1] for n in systems]
    levels = size.bit_length() - 2
    for level in range(levels):
        mask = masks[2 + level]
        mid = [dot(n * mask, t).astype(BF16) for n, t in zip(systems, out)]
        out = [t - dot(t, m).astype(BF16) for t, m in zip(out, mid)]
    return out


def level_masks(size):
    row = lax.broadcasted_iota(jnp.int32, (size, size), 0)
    col = lax.broadcasted_iota(jnp.int32, (size, size), 1)
    lower = row > col
    masks = [(row == col)]
    for level in range(size.bit_length() - 1):
        same = (row >> (level + 1)) == (col >> (level + 1))
        apart = (row >> level) != (col >> level)
        masks.append(lower & same & apart)
    return [m.astype(F32).astype(BF16) for m in masks]


def layer_kernel(
    n_in, n_out, q_ref, k_ref, v_ref, b_ref, gain_ref, mixed_ref,
    mask_ref, maps, zhi, zlo, outs, comp, pre, state, after, relay,
    s_pre, r_pre, s_chain, s_relay, r_state,
):
    heads, size = maps.shape[0], maps.shape[1]
    count, rows = q_ref.shape[0], k_ref.shape[0]
    half = rows // 2
    steps, group = b_ref.shape[0], b_ref.shape[2]
    span = group * size
    at, grp = lax.axis_index("inner"), lax.axis_index("outer")
    first, last = at == 0, at == n_in - 1
    inside = jnp.logical_not(first | last)
    has_prev = grp > 0
    has_next = grp < n_out - 1
    ends = first | last

    barrier = pltpu.get_barrier_semaphore()
    greetings = (
        (at > 0, (grp, at - 1)),
        (at < n_in - 1, (grp, at + 1)),
        (ends & has_prev, (grp - 1, at)),
        (ends & has_next, (grp + 1, at)),
    )
    for cond, dev in greetings:
        @pl.when(cond)
        def _():
            pl.semaphore_signal(barrier, inc=1, device_id=dev, device_id_type=MESH)

    for where, m in enumerate(level_masks(half)):
        mask_ref[where] = m
    pl.semaphore_wait(barrier, sum(c.astype(jnp.int32) for c, _ in greetings))

    def send_pre(h, fwd, src):
        return pltpu.make_async_remote_copy(
            src.at[h], pre.at[h], s_pre.at[h], r_pre.at[h],
            device_id=(grp, at + 1 if fwd else at - 1), device_id_type=MESH)

    def send_chain(h):
        return pltpu.make_async_remote_copy(
            after.at[h], state.at[h], s_chain.at[h], r_state.at[h],
            device_id=(grp + 1, at), device_id_type=MESH)

    def send_relay(h, fwd):
        src = state if fwd else relay
        return pltpu.make_async_remote_copy(
            src.at[h], state.at[h], s_relay.at[h], r_state.at[h],
            device_id=(grp, at - 1 if fwd else at + 1), device_id_type=MESH)

    row_h = lax.broadcasted_iota(jnp.int32, (half, half), 0)
    col_h = lax.broadcasted_iota(jnp.int32, (half, half), 1)
    span_of = [slice(h * size, (h + 1) * size) for h in range(group)]

    def lanes(step):
        return pl.ds(pl.multiple_of(step * span, span), span)

    def make_maps(step):
        masks = [mask_ref[m] for m in range(mask_ref.shape[0])]
        strict = row_h > col_h
        eye = (row_h == col_h).astype(F32)
        beta_all = 2.0 / (1.0 + jnp.exp(-b_ref[step]))
        k_all, v_all = k_ref[:, lanes(step)], v_ref[:, lanes(step)]
        k = [k_all[:, c] for c in span_of]
        n00, n10, n11, rhs = [], [], [], []
        for h in range(group):
            kf = k[h].astype(F32)
            inv = 1.0 / (jnp.sum(kf * kf, axis=-1, keepdims=True) + 1e-06)
            beta = beta_all[:, h : h + 1]
            coef = beta * inv
            k0, k1 = k[h][:half], k[h][half:]
            n00.append(split(jnp.where(strict, coef[:half] * dot_nt(k0, k0), 0.0)))
            n11.append(split(jnp.where(strict, coef[half:] * dot_nt(k1, k1), 0.0)))
            n10.append(split(coef[half:] * dot_nt(k1, k0)))
            vf = v_all[:, span_of[h]].astype(F32) * (beta * jnp.sqrt(inv))
            rhs.append(jnp.concatenate([vf, kf * coef], axis=1))
        inverse = unit_lower_inverses([n[0] for n in n00] + [n[0] for n in n11], masks)

        def solve(t, n, r):
            zh = dot(t, r.astype(BF16)).astype(BF16)
            res = (r - zh.astype(F32)) - (dot(n[0], zh) + dot(n[1], zh))
            return zh, dot(t, res.astype(BF16)).astype(BF16)

        top = [solve(inverse[h], n00[h], rhs[h][:half]) for h in range(group)]
        low = []
        for h in range(group):
            th, tl = top[h]
            r = rhs[h][half:] - (dot(n10[h][0], th) + (dot(n10[h][1], th) + dot(n10[h][0], tl)))
            low.append(solve(inverse[group + h], n11[h], r))
        for h in range(group):
            head = step * group + h
            zh = jnp.concatenate([top[h][0], low[h][0]], axis=0)
            zl = jnp.concatenate([top[h][1], low[h][1]], axis=0)
            kz = dot_tn(k[h], zh) + dot_tn(k[h], zl)
            maps[head, :, :size] = eye - kz[:, size:]
            maps[head, :, size:] = kz[:, :size]
            zhi[head] = zh
            zlo[head] = zl

    def make_outs(step):
        tok = lax.broadcasted_iota(jnp.int32, (count, rows), 0)
        virt = lax.broadcasted_iota(jnp.int32, (count, rows), 1)
        seen = virt <= 2 * tok + 1
        k_all, q_all = k_ref[:, lanes(step)], q_ref[:, lanes(step)]
        for h in range(group):
            head = step * group + h
            q = q_all[:, span_of[h]]
            qf = q.astype(F32)
            rq = lax.rsqrt(jnp.sum(qf * qf, axis=-1, keepdims=True) + 1e-06)
            ph, plo = split(jnp.where(seen, dot_nt(q, k_all[:, span_of[h]]), 0.0))
            zh = zhi[head]
            pz = dot(ph, zh) + (dot(plo, zh) + dot(ph, zlo[head]))
            outs[head, :, :size] = pz[:, :size] * rq
            outs[head, :, size:] = (qf - pz[:, size:]) * rq

    def prefix(h, fwd):
        start, end = (first, last) if fwd else (last, first)

        @pl.when(start)
        def _():
            send_pre(h, fwd, maps).start()

        @pl.when(jnp.logical_not(start))
        def _():
            send_pre(h, fwd, comp).wait_recv()
            own, got = maps[h], pre[h]
            late, early = (own, got) if fwd else (got, own)
            both = dot3(late[:, :size], early)
            comp[h, :, :size] = both[:, :size]
            comp[h, :, size:] = both[:, size:] + late[:, size:]

            @pl.when(jnp.logical_not(end))
            def _():
                send_pre(h, fwd, comp).start()

    def sweep(t, _):
        @pl.when(t < steps)
        def _():
            make_maps(t)

        @pl.when((t >= steps) & (t < 2 * steps))
        def _():
            make_outs(t - steps)

        fwd_step, bwd_step = t - 2 * at, t - 2 * (n_in - 1 - at)
        for pair in range(group // 2):
            @pl.when((fwd_step >= 0) & (fwd_step < steps))
            def _():
                prefix(fwd_step * group + 2 * pair, True)

            @pl.when((bwd_step >= 0) & (bwd_step < steps))
            def _():
                prefix(bwd_step * group + 2 * pair + 1, False)

        return 0

    lax.fori_loop(0, max(2 * steps, steps + 2 * (n_in - 1)), sweep, 0)

    def advance(src, h):
        return dot3(src[h, :, :size], state[h]) + src[h, :, size:]

    def link(j, _):
        for fwd in (True, False):
            h = 2 * j + (0 if fwd else 1)
            end = last if fwd else first

            @pl.when(end & has_prev)
            def _():
                send_chain(h).wait_recv()

            @pl.when(end & jnp.logical_not(has_prev))
            def _():
                state[h] = jnp.zeros((size, size), F32)

            @pl.when(end & has_next)
            def _():
                after[h] = advance(comp, h)
                send_chain(h).start()

            @pl.when(end)
            def _():
                if not fwd:
                    relay[h] = advance(maps, h)
                send_relay(h, fwd).start()

        return 0

    @pl.when(ends)
    def _():
        lax.fori_loop(0, heads // 2, link, 0)

    def finish(j, _):
        for fwd in (True, False):
            h = 2 * j + (0 if fwd else 1)
            start, end = (first, last) if fwd else (last, first)

            @pl.when(jnp.logical_not(end))
            def _():
                send_relay(h, fwd).wait_recv()

            @pl.when(inside)
            def _():
                if not fwd:
                    relay[h] = advance(maps, h)
                send_relay(h, fwd).start()

            def emit(entry):
                full = outs[h, :, :size] + dot3(outs[h, :, size:], entry)
                scale = lax.rsqrt(jnp.mean(full * full, axis=-1, keepdims=True) + 1e-06)
                where = pl.ds(pl.multiple_of(h * size, size), size)
                mixed_ref[:, where] = (full * scale * gain_ref[:, where]).astype(BF16)

            if fwd:
                @pl.when(start)
                def _():
                    emit(state[h])

                @pl.when(jnp.logical_not(start))
                def _():
                    emit(advance(pre, h))
            else:
                emit(state[h])

        return 0

    lax.fori_loop(0, heads // 2, finish, 0)

    def drain(j, _):
        for fwd in (True, False):
            h = 2 * j + (0 if fwd else 1)
            start, end = (first, last) if fwd else (last, first)

            @pl.when(jnp.logical_not(end))
            def _():
                send_pre(h, fwd, comp).wait_send()

            @pl.when(end & has_next)
            def _():
                send_chain(h).wait_send()

            @pl.when(jnp.logical_not(start))
            def _():
                send_relay(h, fwd).wait_send()

        return 0

    lax.fori_loop(0, heads // 2, drain, 0)


def local(queries, keys, values, beta_logit, gain):
    count, width = queries.shape
    heads = beta_logit.shape[1]
    size = width // heads
    rows = 2 * count
    steps = heads // GROUP
    half = rows // 2
    n_in, n_out = lax.axis_size("inner"), lax.axis_size("outer")
    k2 = keys.reshape(rows, width)
    v2 = values.reshape(rows, width)
    b2 = beta_logit.transpose(1, 2, 0).reshape(steps, GROUP, rows).transpose(0, 2, 1)
    vmem = pl.BlockSpec(memory_space=pltpu.VMEM)
    sems = pltpu.SemaphoreType.DMA((heads,))
    wide = pltpu.VMEM((heads, size, 2 * size), F32)
    square = pltpu.VMEM((heads, size, size), F32)
    solved = pltpu.VMEM((heads, rows, 2 * size), BF16)
    return pl.pallas_call(
        functools.partial(layer_kernel, n_in, n_out),
        out_shape=jax.ShapeDtypeStruct((count, width), BF16),
        in_specs=[vmem] * 5,
        out_specs=vmem,
        scratch_shapes=[
            pltpu.VMEM((half.bit_length(), half, half), BF16),
            wide, solved, solved,
            pltpu.VMEM((heads, count, 2 * size), F32),
            wide, wide, square, square, square,
            sems, sems, sems, sems, sems,
        ],
        compiler_params=pltpu.CompilerParams(
            collective_id=0, has_side_effects=True, vmem_limit_bytes=48 * 1024 * 1024
        ),
    )(queries, k2, v2, b2, gain.reshape(1, -1))


def solution(mesh):
    return jax.shard_map(
        local,
        mesh=mesh,
        in_specs=(
            P(("outer", "inner"), None),
            P(("outer", "inner"), None, None),
            P(("outer", "inner"), None, None),
            P(None, None, ("outer", "inner")),
            P(),
        ),
        out_specs=P(("outer", "inner"), None),
        check_vma=False,
    )
```

```python
import functools

import jax
import jax.numpy as jnp
from jax import lax
from jax.experimental import pallas as pl
from jax.experimental.pallas import tpu as pltpu
from jax.sharding import PartitionSpec as P

F32 = jnp.float32
BF16 = jnp.bfloat16
MESH = pl.DeviceIdType.MESH
GROUP = 2


def dot(a, b):
    return lax.dot_general(a, b, (((1,), (0,)), ((), ())), preferred_element_type=F32)


def dot_nt(a, b):
    return lax.dot_general(a, b, (((1,), (1,)), ((), ())), preferred_element_type=F32)


def dot_tn(a, b):
    return lax.dot_general(a, b, (((0,), (0,)), ((), ())), preferred_element_type=F32)


def split(x):
    hi = x.astype(BF16)
    return hi, (x - hi.astype(F32)).astype(BF16)


def dot3(a, b):
    ah, al = split(a)
    bh, bl = split(b)
    return dot(ah, bh) + (dot(ah, bl) + dot(al, bh))


def unit_lower_inverses(systems, masks):
    size = systems[0].shape[0]
    eye = masks[0]
    out = [eye - n * masks[1] for n in systems]
    levels = size.bit_length() - 2
    for level in range(levels):
        mask = masks[2 + level]
        mid = [dot(n * mask, t).astype(BF16) for n, t in zip(systems, out)]
        out = [t - dot(t, m).astype(BF16) for t, m in zip(out, mid)]
    return out


def level_masks(size):
    row = lax.broadcasted_iota(jnp.int32, (size, size), 0)
    col = lax.broadcasted_iota(jnp.int32, (size, size), 1)
    lower = row > col
    masks = [(row == col)]
    for level in range(size.bit_length() - 1):
        same = (row >> (level + 1)) == (col >> (level + 1))
        apart = (row >> level) != (col >> level)
        masks.append(lower & same & apart)
    return [m.astype(F32).astype(BF16) for m in masks]


def layer_kernel(
    n_in, n_out, q_ref, k_ref, v_ref, b_ref, gain_ref, mixed_ref,
    mask_ref, maps, zhi, zlo, outs, comp, pre, state, after, relay,
    s_pre, r_pre, s_chain, s_relay, r_state,
):
    heads, size = maps.shape[0], maps.shape[1]
    count, rows = q_ref.shape[0], k_ref.shape[0]
    half = rows // 2
    steps, group = b_ref.shape[0], b_ref.shape[2]
    span = group * size
    at, grp = lax.axis_index("inner"), lax.axis_index("outer")
    first, last = at == 0, at == n_in - 1
    has_prev = grp > 0
    has_next = grp < n_out - 1
    ends = first | last

    barrier = pltpu.get_barrier_semaphore()
    greetings = (
        (at > 0, (grp, at - 1)),
        (at < n_in - 1, (grp, at + 1)),
        (ends & has_prev, (grp - 1, at)),
        (ends & has_next, (grp + 1, at)),
    )
    for cond, dev in greetings:
        @pl.when(cond)
        def _():
            pl.semaphore_signal(barrier, inc=1, device_id=dev, device_id_type=MESH)

    for where, m in enumerate(level_masks(half)):
        mask_ref[where] = m
    pl.semaphore_wait(barrier, sum(c.astype(jnp.int32) for c, _ in greetings))

    def send_pre(h, fwd, src):
        return pltpu.make_async_remote_copy(
            src.at[h], pre.at[h], s_pre.at[h], r_pre.at[h],
            device_id=(grp, at + 1 if fwd else at - 1), device_id_type=MESH)

    def send_chain(h):
        return pltpu.make_async_remote_copy(
            after.at[h], state.at[h], s_chain.at[h], r_state.at[h],
            device_id=(grp + 1, at), device_id_type=MESH)

    def send_relay(h, fwd):
        src = state if fwd else relay
        return pltpu.make_async_remote_copy(
            src.at[h], state.at[h], s_relay.at[h], r_state.at[h],
            device_id=(grp, at - 1 if fwd else at + 1), device_id_type=MESH)

    row_h = lax.broadcasted_iota(jnp.int32, (half, half), 0)
    col_h = lax.broadcasted_iota(jnp.int32, (half, half), 1)
    span_of = [slice(h * size, (h + 1) * size) for h in range(group)]

    def lanes(step):
        return pl.ds(pl.multiple_of(step * span, span), span)

    def make_maps(step):
        masks = [mask_ref[m] for m in range(mask_ref.shape[0])]
        strict = row_h > col_h
        eye = (row_h == col_h).astype(F32)
        beta_all = 2.0 / (1.0 + jnp.exp(-b_ref[step]))
        k_all, v_all = k_ref[:, lanes(step)], v_ref[:, lanes(step)]
        k = [k_all[:, c] for c in span_of]
        n00, n10, n11, rhs = [], [], [], []
        for h in range(group):
            kf = k[h].astype(F32)
            inv = 1.0 / (jnp.sum(kf * kf, axis=-1, keepdims=True) + 1e-06)
            beta = beta_all[:, h : h + 1]
            coef = beta * inv
            k0, k1 = k[h][:half], k[h][half:]
            n00.append(split(jnp.where(strict, coef[:half] * dot_nt(k0, k0), 0.0)))
            n11.append(split(jnp.where(strict, coef[half:] * dot_nt(k1, k1), 0.0)))
            n10.append(split(coef[half:] * dot_nt(k1, k0)))
            vf = v_all[:, span_of[h]].astype(F32) * (beta * jnp.sqrt(inv))
            rhs.append(jnp.concatenate([vf, kf * coef], axis=1))
        inverse = unit_lower_inverses([n[0] for n in n00] + [n[0] for n in n11], masks)

        def solve(t, n, r):
            zh = dot(t, r.astype(BF16)).astype(BF16)
            res = (r - zh.astype(F32)) - (dot(n[0], zh) + dot(n[1], zh))
            return zh, dot(t, res.astype(BF16)).astype(BF16)

        top = [solve(inverse[h], n00[h], rhs[h][:half]) for h in range(group)]
        low = []
        for h in range(group):
            th, tl = top[h]
            r = rhs[h][half:] - (dot(n10[h][0], th) + (dot(n10[h][1], th) + dot(n10[h][0], tl)))
            low.append(solve(inverse[group + h], n11[h], r))
        for h in range(group):
            head = step * group + h
            zh = jnp.concatenate([top[h][0], low[h][0]], axis=0)
            zl = jnp.concatenate([top[h][1], low[h][1]], axis=0)
            kz = dot_tn(k[h], zh) + dot_tn(k[h], zl)
            maps[head, :, :size] = eye - kz[:, size:]
            maps[head, :, size:] = kz[:, :size]
            zhi[h] = zh
            zlo[h] = zl

    def make_outs(step):
        tok = lax.broadcasted_iota(jnp.int32, (count, rows), 0)
        virt = lax.broadcasted_iota(jnp.int32, (count, rows), 1)
        seen = virt <= 2 * tok + 1
        k_all, q_all = k_ref[:, lanes(step)], q_ref[:, lanes(step)]
        for h in range(group):
            head = step * group + h
            q = q_all[:, span_of[h]]
            qf = q.astype(F32)
            rq = lax.rsqrt(jnp.sum(qf * qf, axis=-1, keepdims=True) + 1e-06)
            ph, plo = split(jnp.where(seen, dot_nt(q, k_all[:, span_of[h]]), 0.0))
            zh = zhi[h]
            pz = dot(ph, zh) + (dot(plo, zh) + dot(ph, zlo[h]))
            outs[head, :, :size] = pz[:, :size] * rq
            outs[head, :, size:] = (qf - pz[:, size:]) * rq

    def prefix(h, fwd):
        start, end = (first, last) if fwd else (last, first)

        @pl.when(start)
        def _():
            send_pre(h, fwd, maps).start()

        @pl.when(jnp.logical_not(start))
        def _():
            send_pre(h, fwd, comp).wait_recv()
            own, got = maps[h], pre[h]
            late, early = (own, got) if fwd else (got, own)
            both = dot3(late[:, :size], early)
            comp[h, :, :size] = both[:, :size]
            comp[h, :, size:] = both[:, size:] + late[:, size:]

            @pl.when(jnp.logical_not(end))
            def _():
                send_pre(h, fwd, comp).start()

    def advance(src, h):
        return dot3(src[h, :, :size], state[h]) + src[h, :, size:]

    def enter(h, fwd):
        end = last if fwd else first

        @pl.when(end & has_prev)
        def _():
            send_chain(h).wait_recv()

        @pl.when(end & jnp.logical_not(has_prev))
        def _():
            state[h] = jnp.zeros((size, size), F32)

        @pl.when(end & has_next)
        def _():
            after[h] = advance(comp, h)
            send_chain(h).start()

        @pl.when(jnp.logical_not(end))
        def _():
            send_relay(h, fwd).wait_recv()

        @pl.when(jnp.logical_not(first if fwd else last))
        def _():
            if not fwd:
                relay[h] = advance(maps, h)
            send_relay(h, fwd).start()

    def emit(h, fwd):
        def write(entry):
            full = outs[h, :, :size] + dot3(outs[h, :, size:], entry)
            scale = lax.rsqrt(jnp.mean(full * full, axis=-1, keepdims=True) + 1e-06)
            where = pl.ds(pl.multiple_of(h * size, size), size)
            mixed_ref[:, where] = (full * scale * gain_ref[:, where]).astype(BF16)

        if fwd:
            @pl.when(first)
            def _():
                write(state[h])

            @pl.when(jnp.logical_not(first))
            def _():
                write(advance(pre, h))
        else:
            write(state[h])

    back = n_in - 1 - at
    shift = n_in + grp // 2
    pairs = (
        (0, True, jnp.where(first, 0, at + 1), shift + back),
        (1, False, jnp.where(last, 0, back + 1), shift + at),
    )

    def sweep(t, _):
        @pl.when(t < steps)
        def _():
            make_maps(t)

        for off, fwd, skew, _ in pairs:
            @pl.when((t >= skew) & (t < steps + skew))
            def _():
                prefix((t - skew) * 2 + off, fwd)

        for off, fwd, _, skew in pairs:
            @pl.when((t >= skew) & (t < steps + skew))
            def _():
                enter((t - skew) * 2 + off, fwd)

        @pl.when(t < steps)
        def _():
            make_outs(t)

        for off, fwd, _, skew in pairs:
            @pl.when((t >= skew) & (t < steps + skew))
            def _():
                emit((t - skew) * 2 + off, fwd)

        return 0

    lax.fori_loop(0, steps + 2 * n_in + n_out // 2, sweep, 0)

    def drain(j, _):
        for fwd in (True, False):
            h = 2 * j + (0 if fwd else 1)
            start, end = (first, last) if fwd else (last, first)

            @pl.when(jnp.logical_not(end))
            def _():
                send_pre(h, fwd, comp).wait_send()

            @pl.when(end & has_next)
            def _():
                send_chain(h).wait_send()

            @pl.when(jnp.logical_not(start))
            def _():
                send_relay(h, fwd).wait_send()

        return 0

    lax.fori_loop(0, heads // 2, drain, 0)


def local(queries, keys, values, beta_logit, gain):
    count, width = queries.shape
    heads = beta_logit.shape[1]
    size = width // heads
    rows = 2 * count
    steps = heads // GROUP
    half = rows // 2
    n_in, n_out = lax.axis_size("inner"), lax.axis_size("outer")
    k2 = keys.reshape(rows, width)
    v2 = values.reshape(rows, width)
    b2 = beta_logit.transpose(1, 2, 0).reshape(steps, GROUP, rows).transpose(0, 2, 1)
    vmem = pl.BlockSpec(memory_space=pltpu.VMEM)
    sems = pltpu.SemaphoreType.DMA((heads,))
    wide = pltpu.VMEM((heads, size, 2 * size), F32)
    square = pltpu.VMEM((heads, size, size), F32)
    solved = pltpu.VMEM((GROUP, rows, 2 * size), BF16)
    return pl.pallas_call(
        functools.partial(layer_kernel, n_in, n_out),
        out_shape=jax.ShapeDtypeStruct((count, width), BF16),
        in_specs=[vmem] * 5,
        out_specs=vmem,
        scratch_shapes=[
            pltpu.VMEM((half.bit_length(), half, half), BF16),
            wide, solved, solved,
            pltpu.VMEM((heads, count, 2 * size), F32),
            wide, wide, square, square, square,
            sems, sems, sems, sems, sems,
        ],
        compiler_params=pltpu.CompilerParams(
            collective_id=0, has_side_effects=True, vmem_limit_bytes=48 * 1024 * 1024
        ),
    )(queries, k2, v2, b2, gain.reshape(1, -1))


def solution(mesh):
    return jax.shard_map(
        local,
        mesh=mesh,
        in_specs=(
            P(("outer", "inner"), None),
            P(("outer", "inner"), None, None),
            P(("outer", "inner"), None, None),
            P(None, None, ("outer", "inner")),
            P(),
        ),
        out_specs=P(("outer", "inner"), None),
        check_vma=False,
    )
```

```python
import functools

import jax
import jax.numpy as jnp
from jax import lax
from jax.experimental import pallas as pl
from jax.experimental.pallas import tpu as pltpu
from jax.sharding import PartitionSpec as P

F32 = jnp.float32
BF16 = jnp.bfloat16
MESH = pl.DeviceIdType.MESH
GROUP = 4


def dot(a, b):
    return lax.dot_general(a, b, (((1,), (0,)), ((), ())), preferred_element_type=F32)


def dot_nt(a, b):
    return lax.dot_general(a, b, (((1,), (1,)), ((), ())), preferred_element_type=F32)


def dot_tn(a, b):
    return lax.dot_general(a, b, (((0,), (0,)), ((), ())), preferred_element_type=F32)


def split(x):
    hi = x.astype(BF16)
    return hi, (x - hi.astype(F32)).astype(BF16)


def dot3(a, b):
    ah, al = split(a)
    bh, bl = split(b)
    return dot(ah, bh) + (dot(ah, bl) + dot(al, bh))


def unit_lower_inverses(systems, masks):
    size = systems[0].shape[0]
    eye = masks[0]
    out = [eye - n * masks[1] for n in systems]
    levels = size.bit_length() - 2
    for level in range(levels):
        mask = masks[2 + level]
        mid = [dot(n * mask, t).astype(BF16) for n, t in zip(systems, out)]
        out = [t - dot(t, m).astype(BF16) for t, m in zip(out, mid)]
    return out


def level_masks(size):
    row = lax.broadcasted_iota(jnp.int32, (size, size), 0)
    col = lax.broadcasted_iota(jnp.int32, (size, size), 1)
    lower = row > col
    masks = [(row == col)]
    for level in range(size.bit_length() - 1):
        same = (row >> (level + 1)) == (col >> (level + 1))
        apart = (row >> level) != (col >> level)
        masks.append(lower & same & apart)
    return [m.astype(F32).astype(BF16) for m in masks]


def layer_kernel(
    n_in, n_out, q_ref, k_ref, v_ref, b_ref, gain_ref, mixed_ref,
    mask_ref, beta_ref, maps, zhi, zlo, outs, comp, pre, state, after, relay,
    s_pre, r_pre, s_chain, s_relay, r_state,
):
    heads, size = maps.shape[0], maps.shape[1]
    count, rows = q_ref.shape[0], k_ref.shape[0]
    half = rows // 2
    steps, group = beta_ref.shape[0], beta_ref.shape[2]
    n_pairs, pairs_at_once = heads // 2, group // 2
    span = group * size
    at, grp = lax.axis_index("inner"), lax.axis_index("outer")
    first, last = at == 0, at == n_in - 1
    has_prev = grp > 0
    has_next = grp < n_out - 1
    ends = first | last

    barrier = pltpu.get_barrier_semaphore()
    greetings = (
        (at > 0, (grp, at - 1)),
        (at < n_in - 1, (grp, at + 1)),
        (ends & has_prev, (grp - 1, at)),
        (ends & has_next, (grp + 1, at)),
    )
    for cond, dev in greetings:
        @pl.when(cond)
        def _():
            pl.semaphore_signal(barrier, inc=1, device_id=dev, device_id_type=MESH)

    for where, m in enumerate(level_masks(half)):
        mask_ref[where] = m
    spot = lax.broadcasted_iota(jnp.int32, (rows, count), 0)
    token = lax.broadcasted_iota(jnp.int32, (rows, count), 1)
    spread = jnp.zeros((rows, heads), F32)
    for j in range(2):
        pick = (spot == 2 * token + j).astype(F32).astype(BF16)
        strength = 2.0 / (1.0 + jnp.exp(-b_ref[j]))
        for _ in range(3):
            part = strength.astype(BF16)
            strength = strength - part.astype(F32)
            spread = spread + dot_nt(pick, part)
    for step in range(steps):
        beta_ref[step] = spread[:, step * group : (step + 1) * group]
    pl.semaphore_wait(barrier, sum(c.astype(jnp.int32) for c, _ in greetings))

    def send_pre(h, fwd, src):
        return pltpu.make_async_remote_copy(
            src.at[h], pre.at[h], s_pre.at[h], r_pre.at[h],
            device_id=(grp, at + 1 if fwd else at - 1), device_id_type=MESH)

    def send_chain(h):
        return pltpu.make_async_remote_copy(
            after.at[h], state.at[h], s_chain.at[h], r_state.at[h],
            device_id=(grp + 1, at), device_id_type=MESH)

    def send_relay(h, fwd):
        src = state if fwd else relay
        return pltpu.make_async_remote_copy(
            src.at[h], state.at[h], s_relay.at[h], r_state.at[h],
            device_id=(grp, at - 1 if fwd else at + 1), device_id_type=MESH)

    row_h = lax.broadcasted_iota(jnp.int32, (half, half), 0)
    col_h = lax.broadcasted_iota(jnp.int32, (half, half), 1)
    span_of = [slice(h * size, (h + 1) * size) for h in range(group)]

    def lanes(step):
        return pl.ds(pl.multiple_of(step * span, span), span)

    def make_maps(step):
        masks = [mask_ref[m] for m in range(mask_ref.shape[0])]
        strict = row_h > col_h
        eye = (row_h == col_h).astype(F32)
        beta_all = beta_ref[step]
        k_all, v_all = k_ref[:, lanes(step)], v_ref[:, lanes(step)]
        k = [k_all[:, c] for c in span_of]
        n00, n10, n11, rhs = [], [], [], []
        for h in range(group):
            kf = k[h].astype(F32)
            inv = 1.0 / (jnp.sum(kf * kf, axis=-1, keepdims=True) + 1e-06)
            beta = beta_all[:, h : h + 1]
            coef = beta * inv
            k0, k1 = k[h][:half], k[h][half:]
            n00.append(split(jnp.where(strict, coef[:half] * dot_nt(k0, k0), 0.0)))
            n11.append(split(jnp.where(strict, coef[half:] * dot_nt(k1, k1), 0.0)))
            n10.append(split(coef[half:] * dot_nt(k1, k0)))
            vf = v_all[:, span_of[h]].astype(F32) * (beta * jnp.sqrt(inv))
            rhs.append(jnp.concatenate([vf, kf * coef], axis=1))
        inverse = unit_lower_inverses([n[0] for n in n00] + [n[0] for n in n11], masks)

        def solve(t, n, r):
            zh = dot(t, r.astype(BF16)).astype(BF16)
            res = (r - zh.astype(F32)) - (dot(n[0], zh) + dot(n[1], zh))
            return zh, dot(t, res.astype(BF16)).astype(BF16)

        top = [solve(inverse[h], n00[h], rhs[h][:half]) for h in range(group)]
        low = []
        for h in range(group):
            th, tl = top[h]
            r = rhs[h][half:] - (dot(n10[h][0], th) + (dot(n10[h][1], th) + dot(n10[h][0], tl)))
            low.append(solve(inverse[group + h], n11[h], r))
        for h in range(group):
            head = step * group + h
            zh = jnp.concatenate([top[h][0], low[h][0]], axis=0)
            zl = jnp.concatenate([top[h][1], low[h][1]], axis=0)
            kz = dot_tn(k[h], zh) + dot_tn(k[h], zl)
            maps[head, :, :size] = eye - kz[:, size:]
            maps[head, :, size:] = kz[:, :size]
            zhi[h] = zh
            zlo[h] = zl

    def make_outs(step):
        tok = lax.broadcasted_iota(jnp.int32, (count, rows), 0)
        virt = lax.broadcasted_iota(jnp.int32, (count, rows), 1)
        seen = virt <= 2 * tok + 1
        k_all, q_all = k_ref[:, lanes(step)], q_ref[:, lanes(step)]
        for h in range(group):
            head = step * group + h
            q = q_all[:, span_of[h]]
            qf = q.astype(F32)
            rq = lax.rsqrt(jnp.sum(qf * qf, axis=-1, keepdims=True) + 1e-06)
            ph, plo = split(jnp.where(seen, dot_nt(q, k_all[:, span_of[h]]), 0.0))
            zh = zhi[h]
            pz = dot(ph, zh) + (dot(plo, zh) + dot(ph, zlo[h]))
            outs[head, :, :size] = pz[:, :size] * rq
            outs[head, :, size:] = (qf - pz[:, size:]) * rq

    def prefix(h, fwd):
        start, end = (first, last) if fwd else (last, first)

        @pl.when(start)
        def _():
            send_pre(h, fwd, maps).start()

        @pl.when(jnp.logical_not(start))
        def _():
            send_pre(h, fwd, comp).wait_recv()
            own, got = maps[h], pre[h]
            late, early = (own, got) if fwd else (got, own)
            both = dot3(late[:, :size], early)
            comp[h, :, :size] = both[:, :size]
            comp[h, :, size:] = both[:, size:] + late[:, size:]

            @pl.when(jnp.logical_not(end))
            def _():
                send_pre(h, fwd, comp).start()

    def advance(src, h):
        return dot3(src[h, :, :size], state[h]) + src[h, :, size:]

    def enter(h, fwd):
        end = last if fwd else first

        @pl.when(end & has_prev)
        def _():
            send_chain(h).wait_recv()

        @pl.when(end & jnp.logical_not(has_prev))
        def _():
            state[h] = jnp.zeros((size, size), F32)

        @pl.when(end & has_next)
        def _():
            after[h] = advance(comp, h)
            send_chain(h).start()

        @pl.when(jnp.logical_not(end))
        def _():
            send_relay(h, fwd).wait_recv()

        @pl.when(jnp.logical_not(first if fwd else last))
        def _():
            if not fwd:
                relay[h] = advance(maps, h)
            send_relay(h, fwd).start()

    def emit(j):
        def write(h, entry):
            full = outs[h, :, :size] + dot3(outs[h, :, size:], entry)
            scale = lax.rsqrt(jnp.mean(full * full, axis=-1, keepdims=True) + 1e-06)
            where = pl.ds(pl.multiple_of(h * size, size), size)
            mixed_ref[:, where] = (full * scale * gain_ref[:, where]).astype(BF16)

        write(2 * j + 1, state[2 * j + 1])
        write(2 * j, advance(pre, 2 * j))

    back = n_in - 1 - at
    shift = n_in + grp // 2
    pairs = (
        (0, True, jnp.where(first, 0, at + 1), shift + back),
        (1, False, jnp.where(last, 0, back + 1), shift + at),
    )
    leave = shift + n_in - 1

    @pl.when(first)
    def _():
        unit = jnp.concatenate(
            [(row_h == col_h).astype(F32), jnp.zeros((size, size), F32)], axis=1)
        for j in range(n_pairs):
            pre[2 * j] = unit

    def sweep(t, _):
        part = t % pairs_at_once

        @pl.when((t < n_pairs) & (part == 0))
        def _():
            make_maps(t // pairs_at_once)

        for off, fwd, skew, _ in pairs:
            @pl.when((t >= skew) & (t < n_pairs + skew))
            def _():
                prefix((t - skew) * 2 + off, fwd)

        for off, fwd, _, skew in pairs:
            @pl.when((t >= skew) & (t < n_pairs + skew))
            def _():
                enter((t - skew) * 2 + off, fwd)

        @pl.when((t < n_pairs) & (part == pairs_at_once - 1))
        def _():
            make_outs(t // pairs_at_once)

        @pl.when((t >= leave) & (t < n_pairs + leave))
        def _():
            emit(t - leave)

        return 0

    lax.fori_loop(0, n_pairs + 2 * n_in + n_out // 2, sweep, 0)

    def drain(j, _):
        for fwd in (True, False):
            h = 2 * j + (0 if fwd else 1)
            start, end = (first, last) if fwd else (last, first)

            @pl.when(jnp.logical_not(end))
            def _():
                send_pre(h, fwd, comp).wait_send()

            @pl.when(end & has_next)
            def _():
                send_chain(h).wait_send()

            @pl.when(jnp.logical_not(start))
            def _():
                send_relay(h, fwd).wait_send()

        return 0

    lax.fori_loop(0, heads // 2, drain, 0)


def local(queries, keys, values, beta_logit, gain):
    count, width = queries.shape
    heads = beta_logit.shape[1]
    size = width // heads
    rows = 2 * count
    steps = heads // GROUP
    half = rows // 2
    n_in, n_out = lax.axis_size("inner"), lax.axis_size("outer")
    k2 = keys.reshape(rows, width)
    v2 = values.reshape(rows, width)
    vmem = pl.BlockSpec(memory_space=pltpu.VMEM)
    sems = pltpu.SemaphoreType.DMA((heads,))
    wide = pltpu.VMEM((heads, size, 2 * size), F32)
    square = pltpu.VMEM((heads, size, size), F32)
    solved = pltpu.VMEM((GROUP, rows, 2 * size), BF16)
    return pl.pallas_call(
        functools.partial(layer_kernel, n_in, n_out),
        out_shape=jax.ShapeDtypeStruct((count, width), BF16),
        in_specs=[vmem] * 5,
        out_specs=vmem,
        scratch_shapes=[
            pltpu.VMEM((half.bit_length(), half, half), BF16),
            pltpu.VMEM((steps, rows, GROUP), F32),
            wide, solved, solved,
            pltpu.VMEM((heads, count, 2 * size), F32),
            wide, wide, square, square, square,
            sems, sems, sems, sems, sems,
        ],
        compiler_params=pltpu.CompilerParams(
            collective_id=0, has_side_effects=True, vmem_limit_bytes=48 * 1024 * 1024
        ),
    )(queries, k2, v2, beta_logit, gain.reshape(1, -1))


def solution(mesh):
    return jax.shard_map(
        local,
        mesh=mesh,
        in_specs=(
            P(("outer", "inner"), None),
            P(("outer", "inner"), None, None),
            P(("outer", "inner"), None, None),
            P(None, None, ("outer", "inner")),
            P(),
        ),
        out_specs=P(("outer", "inner"), None),
        check_vma=False,
    )
```

```python
import functools

import jax
import jax.numpy as jnp
from jax import lax
from jax.experimental import pallas as pl
from jax.experimental.pallas import tpu as pltpu
from jax.sharding import PartitionSpec as P

F32 = jnp.float32
BF16 = jnp.bfloat16
MESH = pl.DeviceIdType.MESH

def dot(a, b):
    return lax.dot_general(a, b, (((1,), (0,)), ((), ())), preferred_element_type=F32)


def dot_nt(a, b):
    return lax.dot_general(a, b, (((1,), (1,)), ((), ())), preferred_element_type=F32)


def dot_tn(a, b):
    return lax.dot_general(a, b, (((0,), (0,)), ((), ())), preferred_element_type=F32)


def split(x):
    hi = x.astype(BF16)
    return hi, (x - hi.astype(F32)).astype(BF16)


def dot3(a, b):
    ah, al = split(a)
    bh, bl = split(b)
    return dot(ah, bh) + (dot(ah, bl) + dot(al, bh))


def unit_lower_inverses(systems, masks):
    size = systems[0].shape[0]
    eye = masks[0]
    out = [eye - n * masks[1] for n in systems]
    levels = size.bit_length() - 2
    for level in range(levels):
        mask = masks[2 + level]
        mid = [dot(n * mask, t).astype(BF16) for n, t in zip(systems, out)]
        out = [t - dot(t, m).astype(BF16) for t, m in zip(out, mid)]
    return out


def level_masks(size):
    row = lax.broadcasted_iota(jnp.int32, (size, size), 0)
    col = lax.broadcasted_iota(jnp.int32, (size, size), 1)
    lower = row > col
    masks = [(row == col)]
    for level in range(size.bit_length() - 1):
        same = (row >> (level + 1)) == (col >> (level + 1))
        apart = (row >> level) != (col >> level)
        masks.append(lower & same & apart)
    return [m.astype(F32).astype(BF16) for m in masks]


def layer_kernel(
    n_in, n_out, q_ref, k_ref, v_ref, b_ref, gain_ref, mixed_ref,
    mask_ref, beta_ref, maps, zhi, zlo, outs, comp, pre, state, after, relay,
    s_pre, r_pre, s_chain, s_relay, r_state,
):
    heads, size = maps.shape[0], maps.shape[1]
    count, rows = q_ref.shape[0], k_ref.shape[0]
    half = rows // 2
    n_pairs = heads // 2
    at, grp = lax.axis_index("inner"), lax.axis_index("outer")
    first, last = at == 0, at == n_in - 1
    has_prev = grp > 0
    has_next = grp < n_out - 1
    ends = first | last

    barrier = pltpu.get_barrier_semaphore()
    greetings = (
        (at > 0, (grp, at - 1)),
        (at < n_in - 1, (grp, at + 1)),
        (ends & has_prev, (grp - 1, at)),
        (ends & has_next, (grp + 1, at)),
    )
    for cond, dev in greetings:
        @pl.when(cond)
        def _():
            pl.semaphore_signal(barrier, inc=1, device_id=dev, device_id_type=MESH)

    for where, m in enumerate(level_masks(half)):
        mask_ref[where] = m
    spot = lax.broadcasted_iota(jnp.int32, (rows, count), 0)
    token = lax.broadcasted_iota(jnp.int32, (rows, count), 1)
    spread = jnp.zeros((rows, heads), F32)
    for j in range(2):
        pick = (spot == 2 * token + j).astype(F32).astype(BF16)
        strength = 2.0 / (1.0 + jnp.exp(-b_ref[j]))
        for _ in range(3):
            part = strength.astype(BF16)
            strength = strength - part.astype(F32)
            spread = spread + dot_nt(pick, part)
    for j in range(n_pairs):
        beta_ref[j] = spread[:, 2 * j : 2 * j + 2]
    peers = sum(c.astype(jnp.int32) for c, _ in greetings)

    def send_pre(h, fwd, src):
        return pltpu.make_async_remote_copy(
            src.at[h], pre.at[h], s_pre.at[h], r_pre.at[h],
            device_id=(grp, at + 1 if fwd else at - 1), device_id_type=MESH)

    def send_chain(h):
        return pltpu.make_async_remote_copy(
            after.at[h], state.at[h], s_chain.at[h], r_state.at[h],
            device_id=(grp + 1, at), device_id_type=MESH)

    def send_relay(h, fwd):
        src = state if fwd else relay
        return pltpu.make_async_remote_copy(
            src.at[h], state.at[h], s_relay.at[h], r_state.at[h],
            device_id=(grp, at - 1 if fwd else at + 1), device_id_type=MESH)

    row_h = lax.broadcasted_iota(jnp.int32, (half, half), 0)
    col_h = lax.broadcasted_iota(jnp.int32, (half, half), 1)

    def lanes(pair, group):
        return pl.ds(pl.multiple_of(pair * 2 * size, 2 * size), group * size)

    def make_maps(pair, group):
        span_of = [slice(h * size, (h + 1) * size) for h in range(group)]
        masks = [mask_ref[m] for m in range(mask_ref.shape[0])]
        strict = row_h > col_h
        eye = (row_h == col_h).astype(F32)
        beta_pairs = [beta_ref[pair + j] for j in range(group // 2)]
        k_all, v_all = k_ref[:, lanes(pair, group)], v_ref[:, lanes(pair, group)]
        k = [k_all[:, c] for c in span_of]
        n00, n10, n11, rhs = [], [], [], []
        for h in range(group):
            kf = k[h].astype(F32)
            inv = 1.0 / (jnp.sum(kf * kf, axis=-1, keepdims=True) + 1e-06)
            beta = beta_pairs[h // 2][:, h % 2 : h % 2 + 1]
            coef = beta * inv
            k0, k1 = k[h][:half], k[h][half:]
            n00.append(split(jnp.where(strict, coef[:half] * dot_nt(k0, k0), 0.0)))
            n11.append(split(jnp.where(strict, coef[half:] * dot_nt(k1, k1), 0.0)))
            n10.append(split(coef[half:] * dot_nt(k1, k0)))
            vf = v_all[:, span_of[h]].astype(F32) * (beta * jnp.sqrt(inv))
            rhs.append(jnp.concatenate([vf, kf * coef], axis=1))
        inverse = unit_lower_inverses([n[0] for n in n00] + [n[0] for n in n11], masks)

        def solve(t, n, r):
            zh = dot(t, r.astype(BF16)).astype(BF16)
            res = (r - zh.astype(F32)) - (dot(n[0], zh) + dot(n[1], zh))
            return zh, dot(t, res.astype(BF16)).astype(BF16)

        top = [solve(inverse[h], n00[h], rhs[h][:half]) for h in range(group)]
        low = []
        for h in range(group):
            th, tl = top[h]
            r = rhs[h][half:] - (dot(n10[h][0], th) + (dot(n10[h][1], th) + dot(n10[h][0], tl)))
            low.append(solve(inverse[group + h], n11[h], r))
        for h in range(group):
            head = 2 * pair + h
            zh = jnp.concatenate([top[h][0], low[h][0]], axis=0)
            zl = jnp.concatenate([top[h][1], low[h][1]], axis=0)
            kz = dot_tn(k[h], zh) + dot_tn(k[h], zl)
            maps[head, :, :size] = eye - kz[:, size:]
            maps[head, :, size:] = kz[:, :size]
            zhi[head] = zh
            zlo[head] = zl

    def make_outs(pair, group):
        span_of = [slice(h * size, (h + 1) * size) for h in range(group)]
        tok = lax.broadcasted_iota(jnp.int32, (count, rows), 0)
        virt = lax.broadcasted_iota(jnp.int32, (count, rows), 1)
        seen = virt <= 2 * tok + 1
        k_all, q_all = k_ref[:, lanes(pair, group)], q_ref[:, lanes(pair, group)]
        for h in range(group):
            head = 2 * pair + h
            q = q_all[:, span_of[h]]
            qf = q.astype(F32)
            rq = lax.rsqrt(jnp.sum(qf * qf, axis=-1, keepdims=True) + 1e-06)
            ph, plo = split(jnp.where(seen, dot_nt(q, k_all[:, span_of[h]]), 0.0))
            zh = zhi[head]
            pz = dot(ph, zh) + (dot(plo, zh) + dot(ph, zlo[head]))
            outs[head, :, :size] = pz[:, :size] * rq
            outs[head, :, size:] = (qf - pz[:, size:]) * rq

    def prefix(h, fwd):
        start, end = (first, last) if fwd else (last, first)

        @pl.when(start)
        def _():
            send_pre(h, fwd, maps).start()

        @pl.when(jnp.logical_not(start))
        def _():
            send_pre(h, fwd, comp).wait_recv()
            own, got = maps[h], pre[h]
            late, early = (own, got) if fwd else (got, own)
            both = dot3(late[:, :size], early)
            comp[h, :, :size] = both[:, :size]
            comp[h, :, size:] = both[:, size:] + late[:, size:]

            @pl.when(jnp.logical_not(end))
            def _():
                send_pre(h, fwd, comp).start()

    def advance(src, h):
        return dot3(src[h, :, :size], state[h]) + src[h, :, size:]

    def chain(h, fwd):
        @pl.when(has_prev)
        def _():
            send_chain(h).wait_recv()

        @pl.when(jnp.logical_not(has_prev))
        def _():
            state[h] = jnp.zeros((size, size), F32)

        @pl.when(has_next)
        def _():
            after[h] = advance(comp, h)
            send_chain(h).start()

    def hand(h, fwd):
        @pl.when(jnp.logical_not(last if fwd else first))
        def _():
            send_relay(h, fwd).wait_recv()

        @pl.when(jnp.logical_not(first if fwd else last))
        def _():
            if not fwd:
                relay[h] = advance(maps, h)
            send_relay(h, fwd).start()

    def emit(j):
        def write(h, entry):
            full = outs[h, :, :size] + dot3(outs[h, :, size:], entry)
            scale = lax.rsqrt(jnp.mean(full * full, axis=-1, keepdims=True) + 1e-06)
            where = pl.ds(pl.multiple_of(h * size, size), size)
            mixed_ref[:, where] = (full * scale * gain_ref[:, where]).astype(BF16)

        write(2 * j + 1, state[2 * j + 1])
        write(2 * j, advance(pre, 2 * j))

    back = n_in - 1 - at
    shift = grp // 2
    pairs = (
        (0, True, jnp.where(first, 0, at + 1), last, back),
        (1, False, jnp.where(last, 0, back + 1), first, at),
    )

    def handed(t):
        early, late = t - n_in + 1, 2 * (t - n_pairs) + 2
        return jnp.clip(jnp.minimum(early, late), 0, n_pairs)

    @pl.when(first)
    def _():
        unit = jnp.concatenate(
            [(row_h == col_h).astype(F32), jnp.zeros((size, size), F32)], axis=1)
        for j in range(n_pairs):
            pre[2 * j] = unit

    def sweep(t, _):
        wide = (t % 2 == 0) & (t >= 2) & (t < n_pairs)

        @pl.when(t < 2)
        def _():
            make_maps(t, 2)

        @pl.when(wide)
        def _():
            make_maps(t, 4)

        @pl.when(t == 0)
        def _():
            pl.semaphore_wait(barrier, peers)

        for off, fwd, skew, _, _ in pairs:
            @pl.when((t >= skew) & (t < n_pairs + skew))
            def _():
                prefix((t - skew) * 2 + off, fwd)

        lead = t - n_in - shift
        for off, fwd, _, end, _ in pairs:
            @pl.when(end & (lead >= 0) & (lead < n_pairs))
            def _():
                chain(lead * 2 + off, fwd)

        for off, fwd, _, _, hops in pairs:
            now = t - shift - hops

            def pass_on(j, _):
                hand(2 * j + off, fwd)
                return 0

            lax.fori_loop(handed(now - 1), handed(now), pass_on, 0)

        @pl.when((t % 2 == 1) & (t < n_pairs))
        def _():
            make_outs(t - 1, 4)

        now = t - shift - (n_in - 1)

        def leave(j, _):
            emit(j)
            return 0

        lax.fori_loop(handed(now - 1), handed(now), leave, 0)
        return 0

    lax.fori_loop(0, n_pairs + 2 * n_in + n_out // 2, sweep, 0)

    def drain(j, _):
        for fwd in (True, False):
            h = 2 * j + (0 if fwd else 1)
            start, end = (first, last) if fwd else (last, first)

            @pl.when(jnp.logical_not(end))
            def _():
                send_pre(h, fwd, comp).wait_send()

            @pl.when(end & has_next)
            def _():
                send_chain(h).wait_send()

            @pl.when(jnp.logical_not(start))
            def _():
                send_relay(h, fwd).wait_send()

        return 0

    lax.fori_loop(0, heads // 2, drain, 0)


def local(queries, keys, values, beta_logit, gain):
    count, width = queries.shape
    heads = beta_logit.shape[1]
    size = width // heads
    rows = 2 * count
    half = rows // 2
    n_in, n_out = lax.axis_size("inner"), lax.axis_size("outer")
    k2 = keys.reshape(rows, width)
    v2 = values.reshape(rows, width)
    vmem = pl.BlockSpec(memory_space=pltpu.VMEM)
    sems = pltpu.SemaphoreType.DMA((heads,))
    wide = pltpu.VMEM((heads, size, 2 * size), F32)
    square = pltpu.VMEM((heads, size, size), F32)
    solved = pltpu.VMEM((heads, rows, 2 * size), BF16)
    return pl.pallas_call(
        functools.partial(layer_kernel, n_in, n_out),
        out_shape=jax.ShapeDtypeStruct((count, width), BF16),
        in_specs=[vmem] * 5,
        out_specs=vmem,
        scratch_shapes=[
            pltpu.VMEM((half.bit_length(), half, half), BF16),
            pltpu.VMEM((heads // 2, rows, 2), F32),
            wide, solved, solved,
            pltpu.VMEM((heads, count, 2 * size), F32),
            wide, wide, square, square, square,
            sems, sems, sems, sems, sems,
        ],
        compiler_params=pltpu.CompilerParams(
            collective_id=0, has_side_effects=True, vmem_limit_bytes=48 * 1024 * 1024
        ),
    )(queries, k2, v2, beta_logit, gain.reshape(1, -1))


def solution(mesh):
    return jax.shard_map(
        local,
        mesh=mesh,
        in_specs=(
            P(("outer", "inner"), None),
            P(("outer", "inner"), None, None),
            P(("outer", "inner"), None, None),
            P(None, None, ("outer", "inner")),
            P(),
        ),
        out_specs=P(("outer", "inner"), None),
        check_vma=False,
    )
```

```python
import functools

import jax
import jax.numpy as jnp
from jax import lax
from jax.experimental import pallas as pl
from jax.experimental.pallas import tpu as pltpu
from jax.sharding import PartitionSpec as P

F32 = jnp.float32
BF16 = jnp.bfloat16
MESH = pl.DeviceIdType.MESH
GROUP = 4


def dot(a, b):
    return lax.dot_general(a, b, (((1,), (0,)), ((), ())), preferred_element_type=F32)


def dot_nt(a, b):
    return lax.dot_general(a, b, (((1,), (1,)), ((), ())), preferred_element_type=F32)


def dot_tn(a, b):
    return lax.dot_general(a, b, (((0,), (0,)), ((), ())), preferred_element_type=F32)


def split(x):
    hi = x.astype(BF16)
    return hi, (x - hi.astype(F32)).astype(BF16)


def dot3(a, b):
    ah, al = split(a)
    bh, bl = split(b)
    return dot(ah, bh) + (dot(ah, bl) + dot(al, bh))


def unit_lower_inverses(systems, masks):
    size = systems[0].shape[0]
    eye = masks[0]
    out = [eye - n * masks[1] for n in systems]
    levels = size.bit_length() - 2
    for level in range(levels):
        mask = masks[2 + level]
        mid = [dot(n * mask, t).astype(BF16) for n, t in zip(systems, out)]
        out = [t - dot(t, m).astype(BF16) for t, m in zip(out, mid)]
    return out


def level_masks(size):
    row = lax.broadcasted_iota(jnp.int32, (size, size), 0)
    col = lax.broadcasted_iota(jnp.int32, (size, size), 1)
    lower = row > col
    masks = [(row == col)]
    for level in range(size.bit_length() - 1):
        same = (row >> (level + 1)) == (col >> (level + 1))
        apart = (row >> level) != (col >> level)
        masks.append(lower & same & apart)
    return [m.astype(F32).astype(BF16) for m in masks]


def layer_kernel(
    n_in, n_out, q_ref, k_ref, v_ref, b_ref, gain_ref, mixed_ref,
    mask_ref, beta_ref, maps, zhi, zlo, outs, comp, pre, state, after, relay,
    s_pre, r_pre, s_chain, s_relay, r_state,
):
    heads, size = maps.shape[0], maps.shape[1]
    count, rows = q_ref.shape[0], k_ref.shape[0]
    half = rows // 2
    steps, group = beta_ref.shape[0], beta_ref.shape[2]
    n_pairs, pairs_at_once = heads // 2, group // 2
    span = group * size
    at, grp = lax.axis_index("inner"), lax.axis_index("outer")
    first, last = at == 0, at == n_in - 1
    has_prev = grp > 0
    has_next = grp < n_out - 1
    ends = first | last

    barrier = pltpu.get_barrier_semaphore()
    greetings = (
        (at > 0, (grp, at - 1)),
        (at < n_in - 1, (grp, at + 1)),
        (ends & has_prev, (grp - 1, at)),
        (ends & has_next, (grp + 1, at)),
    )
    for cond, dev in greetings:
        @pl.when(cond)
        def _():
            pl.semaphore_signal(barrier, inc=1, device_id=dev, device_id_type=MESH)

    for where, m in enumerate(level_masks(half)):
        mask_ref[where] = m
    spot = lax.broadcasted_iota(jnp.int32, (rows, count), 0)
    token = lax.broadcasted_iota(jnp.int32, (rows, count), 1)
    spread = jnp.zeros((rows, heads), F32)
    for j in range(2):
        pick = (spot == 2 * token + j).astype(F32).astype(BF16)
        strength = 2.0 / (1.0 + jnp.exp(-b_ref[j]))
        for _ in range(3):
            part = strength.astype(BF16)
            strength = strength - part.astype(F32)
            spread = spread + dot_nt(pick, part)
    for step in range(steps):
        beta_ref[step] = spread[:, step * group : (step + 1) * group]
    peers = sum(c.astype(jnp.int32) for c, _ in greetings)

    def send_pre(h, fwd, src):
        return pltpu.make_async_remote_copy(
            src.at[h], pre.at[h], s_pre.at[h], r_pre.at[h],
            device_id=(grp, at + 1 if fwd else at - 1), device_id_type=MESH)

    def send_chain(h):
        return pltpu.make_async_remote_copy(
            after.at[h], state.at[h], s_chain.at[h], r_state.at[h],
            device_id=(grp + 1, at), device_id_type=MESH)

    def send_relay(h, fwd):
        src = state if fwd else relay
        return pltpu.make_async_remote_copy(
            src.at[h], state.at[h], s_relay.at[h], r_state.at[h],
            device_id=(grp, at - 1 if fwd else at + 1), device_id_type=MESH)

    row_h = lax.broadcasted_iota(jnp.int32, (half, half), 0)
    col_h = lax.broadcasted_iota(jnp.int32, (half, half), 1)
    span_of = [slice(h * size, (h + 1) * size) for h in range(group)]

    def lanes(step):
        return pl.ds(pl.multiple_of(step * span, span), span)

    def make_maps(step):
        masks = [mask_ref[m] for m in range(mask_ref.shape[0])]
        strict = row_h > col_h
        eye = (row_h == col_h).astype(F32)
        beta_all = beta_ref[step]
        k_all, v_all = k_ref[:, lanes(step)], v_ref[:, lanes(step)]
        k = [k_all[:, c] for c in span_of]
        n00, n10, n11, rhs = [], [], [], []
        for h in range(group):
            kf = k[h].astype(F32)
            inv = 1.0 / (jnp.sum(kf * kf, axis=-1, keepdims=True) + 1e-06)
            beta = beta_all[:, h : h + 1]
            coef = beta * inv
            k0, k1 = k[h][:half], k[h][half:]
            n00.append(split(jnp.where(strict, coef[:half] * dot_nt(k0, k0), 0.0)))
            n11.append(split(jnp.where(strict, coef[half:] * dot_nt(k1, k1), 0.0)))
            n10.append(split(coef[half:] * dot_nt(k1, k0)))
            vf = v_all[:, span_of[h]].astype(F32) * (beta * jnp.sqrt(inv))
            rhs.append(jnp.concatenate([vf, kf * coef], axis=1))
        inverse = unit_lower_inverses([n[0] for n in n00] + [n[0] for n in n11], masks)

        def solve(t, n, r):
            zh = dot(t, r.astype(BF16)).astype(BF16)
            res = (r - zh.astype(F32)) - (dot(n[0], zh) + dot(n[1], zh))
            return zh, dot(t, res.astype(BF16)).astype(BF16)

        top = [solve(inverse[h], n00[h], rhs[h][:half]) for h in range(group)]
        low = []
        for h in range(group):
            th, tl = top[h]
            r = rhs[h][half:] - (dot(n10[h][0], th) + (dot(n10[h][1], th) + dot(n10[h][0], tl)))
            low.append(solve(inverse[group + h], n11[h], r))
        for h in range(group):
            head = step * group + h
            zh = jnp.concatenate([top[h][0], low[h][0]], axis=0)
            zl = jnp.concatenate([top[h][1], low[h][1]], axis=0)
            kz = dot_tn(k[h], zh) + dot_tn(k[h], zl)
            maps[head, :, :size] = eye - kz[:, size:]
            maps[head, :, size:] = kz[:, :size]
            zhi[h] = zh
            zlo[h] = zl

    def make_outs(step):
        tok = lax.broadcasted_iota(jnp.int32, (count, rows), 0)
        virt = lax.broadcasted_iota(jnp.int32, (count, rows), 1)
        seen = virt <= 2 * tok + 1
        k_all, q_all = k_ref[:, lanes(step)], q_ref[:, lanes(step)]
        for h in range(group):
            head = step * group + h
            q = q_all[:, span_of[h]]
            qf = q.astype(F32)
            rq = lax.rsqrt(jnp.sum(qf * qf, axis=-1, keepdims=True) + 1e-06)
            ph, plo = split(jnp.where(seen, dot_nt(q, k_all[:, span_of[h]]), 0.0))
            zh = zhi[h]
            pz = dot(ph, zh) + (dot(plo, zh) + dot(ph, zlo[h]))
            outs[head, :, :size] = pz[:, :size] * rq
            outs[head, :, size:] = (qf - pz[:, size:]) * rq

    def prefix(h, fwd):
        start, end = (first, last) if fwd else (last, first)

        @pl.when(start)
        def _():
            send_pre(h, fwd, maps).start()

        @pl.when(jnp.logical_not(start))
        def _():
            send_pre(h, fwd, comp).wait_recv()
            own, got = maps[h], pre[h]
            late, early = (own, got) if fwd else (got, own)
            both = dot3(late[:, :size], early)
            comp[h, :, :size] = both[:, :size]
            comp[h, :, size:] = both[:, size:] + late[:, size:]

            @pl.when(jnp.logical_not(end))
            def _():
                send_pre(h, fwd, comp).start()

    def advance(src, h):
        return dot3(src[h, :, :size], state[h]) + src[h, :, size:]

    def enter(h, fwd):
        end = last if fwd else first

        @pl.when(end & has_prev)
        def _():
            send_chain(h).wait_recv()

        @pl.when(end & jnp.logical_not(has_prev))
        def _():
            state[h] = jnp.zeros((size, size), F32)

        @pl.when(end & has_next)
        def _():
            after[h] = advance(comp, h)
            send_chain(h).start()

        @pl.when(jnp.logical_not(end))
        def _():
            send_relay(h, fwd).wait_recv()

        @pl.when(jnp.logical_not(first if fwd else last))
        def _():
            if not fwd:
                relay[h] = advance(maps, h)
            send_relay(h, fwd).start()

    def emit(j):
        def write(h, entry):
            full = outs[h, :, :size] + dot3(outs[h, :, size:], entry)
            scale = lax.rsqrt(jnp.mean(full * full, axis=-1, keepdims=True) + 1e-06)
            where = pl.ds(pl.multiple_of(h * size, size), size)
            mixed_ref[:, where] = (full * scale * gain_ref[:, where]).astype(BF16)

        write(2 * j + 1, state[2 * j + 1])
        write(2 * j, advance(pre, 2 * j))

    back = n_in - 1 - at
    shift = 2 * (n_in - 1) + grp // 2
    pairs = (
        (0, True, 2 * at, shift + back),
        (1, False, 2 * back, shift + at),
    )
    leave = shift + n_in - 1

    @pl.when(first)
    def _():
        unit = jnp.concatenate(
            [(row_h == col_h).astype(F32), jnp.zeros((size, size), F32)], axis=1)
        for j in range(n_pairs):
            pre[2 * j] = unit

    def sweep(t, _):
        part = t % pairs_at_once

        @pl.when((t < n_pairs) & (part == 0))
        def _():
            make_maps(t // pairs_at_once)

        @pl.when(t == 0)
        def _():
            pl.semaphore_wait(barrier, peers)

        for off, fwd, skew, _ in pairs:
            @pl.when((t >= skew) & (t < n_pairs + skew))
            def _():
                prefix((t - skew) * 2 + off, fwd)

        for off, fwd, _, skew in pairs:
            @pl.when((t >= skew) & (t < n_pairs + skew))
            def _():
                enter((t - skew) * 2 + off, fwd)

        @pl.when((t < n_pairs) & (part == pairs_at_once - 1))
        def _():
            make_outs(t // pairs_at_once)

        @pl.when((t >= leave) & (t < n_pairs + leave))
        def _():
            emit(t - leave)

        return 0

    lax.fori_loop(0, n_pairs + 3 * n_in + n_out // 2, sweep, 0)

    def drain(j, _):
        for fwd in (True, False):
            h = 2 * j + (0 if fwd else 1)
            start, end = (first, last) if fwd else (last, first)

            @pl.when(jnp.logical_not(end))
            def _():
                send_pre(h, fwd, comp).wait_send()

            @pl.when(end & has_next)
            def _():
                send_chain(h).wait_send()

            @pl.when(jnp.logical_not(start))
            def _():
                send_relay(h, fwd).wait_send()

        return 0

    lax.fori_loop(0, heads // 2, drain, 0)


def local(queries, keys, values, beta_logit, gain):
    count, width = queries.shape
    heads = beta_logit.shape[1]
    size = width // heads
    rows = 2 * count
    steps = heads // GROUP
    half = rows // 2
    n_in, n_out = lax.axis_size("inner"), lax.axis_size("outer")
    k2 = keys.reshape(rows, width)
    v2 = values.reshape(rows, width)
    vmem = pl.BlockSpec(memory_space=pltpu.VMEM)
    sems = pltpu.SemaphoreType.DMA((heads,))
    wide = pltpu.VMEM((heads, size, 2 * size), F32)
    square = pltpu.VMEM((heads, size, size), F32)
    solved = pltpu.VMEM((GROUP, rows, 2 * size), BF16)
    return pl.pallas_call(
        functools.partial(layer_kernel, n_in, n_out),
        out_shape=jax.ShapeDtypeStruct((count, width), BF16),
        in_specs=[vmem] * 5,
        out_specs=vmem,
        scratch_shapes=[
            pltpu.VMEM((half.bit_length(), half, half), BF16),
            pltpu.VMEM((steps, rows, GROUP), F32),
            wide, solved, solved,
            pltpu.VMEM((heads, count, 2 * size), F32),
            wide, wide, square, square, square,
            sems, sems, sems, sems, sems,
        ],
        compiler_params=pltpu.CompilerParams(
            collective_id=0, has_side_effects=True, vmem_limit_bytes=48 * 1024 * 1024
        ),
    )(queries, k2, v2, beta_logit, gain.reshape(1, -1))


def solution(mesh):
    return jax.shard_map(
        local,
        mesh=mesh,
        in_specs=(
            P(("outer", "inner"), None),
            P(("outer", "inner"), None, None),
            P(("outer", "inner"), None, None),
            P(None, None, ("outer", "inner")),
            P(),
        ),
        out_specs=P(("outer", "inner"), None),
        check_vma=False,
    )
```

```python
import functools

import jax
import jax.numpy as jnp
from jax import lax
from jax.experimental import pallas as pl
from jax.experimental.pallas import tpu as pltpu
from jax.sharding import PartitionSpec as P

F32 = jnp.float32
BF16 = jnp.bfloat16
MESH = pl.DeviceIdType.MESH
GROUP = 4


def dot(a, b):
    return lax.dot_general(a, b, (((1,), (0,)), ((), ())), preferred_element_type=F32)


def dot_nt(a, b):
    return lax.dot_general(a, b, (((1,), (1,)), ((), ())), preferred_element_type=F32)


def dot_tn(a, b):
    return lax.dot_general(a, b, (((0,), (0,)), ((), ())), preferred_element_type=F32)


def split(x):
    hi = x.astype(BF16)
    return hi, (x - hi.astype(F32)).astype(BF16)


def dot3_split(a, b):
    return dot(a[0], b[0]) + (dot(a[0], b[1]) + dot(a[1], b[0]))


def dot3(a, b):
    return dot3_split(split(a), split(b))


def unit_lower_inverses(systems, masks):
    size = systems[0].shape[0]
    eye = masks[0]
    out = [eye - n * masks[1] for n in systems]
    levels = size.bit_length() - 2
    for level in range(levels):
        mask = masks[2 + level]
        mid = [dot(n * mask, t).astype(BF16) for n, t in zip(systems, out)]
        out = [t - dot(t, m).astype(BF16) for t, m in zip(out, mid)]
    return out


def level_masks(size):
    row = lax.broadcasted_iota(jnp.int32, (size, size), 0)
    col = lax.broadcasted_iota(jnp.int32, (size, size), 1)
    lower = row > col
    masks = [(row == col)]
    for level in range(size.bit_length() - 1):
        same = (row >> (level + 1)) == (col >> (level + 1))
        apart = (row >> level) != (col >> level)
        masks.append(lower & same & apart)
    return [m.astype(F32).astype(BF16) for m in masks]


def layer_kernel(
    n_in, n_out, q_ref, k_ref, v_ref, b_ref, gain_ref, mixed_ref,
    mask_ref, beta_ref, maps, zhi, zlo, outs, comp, pre, state, after, relay,
    s_pre, r_pre, s_chain, s_relay, r_state,
):
    heads, size = maps.shape[0], maps.shape[1]
    count, rows = q_ref.shape[0], k_ref.shape[0]
    half = rows // 2
    steps, group = beta_ref.shape[0], beta_ref.shape[2]
    n_pairs, pairs_at_once = heads // 2, group // 2
    span = group * size
    at, grp = lax.axis_index("inner"), lax.axis_index("outer")
    first, last = at == 0, at == n_in - 1
    has_prev = grp > 0
    has_next = grp < n_out - 1
    ends = first | last

    barrier = pltpu.get_barrier_semaphore()
    greetings = (
        (at > 0, (grp, at - 1)),
        (at < n_in - 1, (grp, at + 1)),
        (ends & has_prev, (grp - 1, at)),
        (ends & has_next, (grp + 1, at)),
    )
    for cond, dev in greetings:
        @pl.when(cond)
        def _():
            pl.semaphore_signal(barrier, inc=1, device_id=dev, device_id_type=MESH)

    for where, m in enumerate(level_masks(half)):
        mask_ref[where] = m
    spot = lax.broadcasted_iota(jnp.int32, (rows, count), 0)
    token = lax.broadcasted_iota(jnp.int32, (rows, count), 1)
    spread = jnp.zeros((rows, heads), F32)
    for j in range(2):
        pick = (spot == 2 * token + j).astype(F32).astype(BF16)
        strength = 2.0 / (1.0 + jnp.exp(-b_ref[j]))
        for _ in range(3):
            part = strength.astype(BF16)
            strength = strength - part.astype(F32)
            spread = spread + dot_nt(pick, part)
    for step in range(steps):
        beta_ref[step] = spread[:, step * group : (step + 1) * group]
    peers = sum(c.astype(jnp.int32) for c, _ in greetings)

    parts = (slice(0, size), slice(size, 2 * size))

    def send_pre(h, fwd, src, piece):
        return pltpu.make_async_remote_copy(
            src.at[h, :, parts[piece]], pre.at[h, :, parts[piece]],
            s_pre.at[h, piece], r_pre.at[h, piece],
            device_id=(grp, at + 1 if fwd else at - 1), device_id_type=MESH)

    def send_chain(h):
        return pltpu.make_async_remote_copy(
            after.at[h], state.at[h], s_chain.at[h], r_state.at[h],
            device_id=(grp + 1, at), device_id_type=MESH)

    def send_relay(h, fwd):
        src = state if fwd else relay
        return pltpu.make_async_remote_copy(
            src.at[h], state.at[h], s_relay.at[h], r_state.at[h],
            device_id=(grp, at - 1 if fwd else at + 1), device_id_type=MESH)

    row_h = lax.broadcasted_iota(jnp.int32, (half, half), 0)
    col_h = lax.broadcasted_iota(jnp.int32, (half, half), 1)
    span_of = [slice(h * size, (h + 1) * size) for h in range(group)]

    def lanes(step):
        return pl.ds(pl.multiple_of(step * span, span), span)

    def make_maps(step):
        masks = [mask_ref[m] for m in range(mask_ref.shape[0])]
        strict = row_h > col_h
        eye = (row_h == col_h).astype(F32)
        beta_all = beta_ref[step]
        k_all, v_all = k_ref[:, lanes(step)], v_ref[:, lanes(step)]
        k = [k_all[:, c] for c in span_of]
        n00, n10, n11, rhs = [], [], [], []
        for h in range(group):
            kf = k[h].astype(F32)
            inv = 1.0 / (jnp.sum(kf * kf, axis=-1, keepdims=True) + 1e-06)
            beta = beta_all[:, h : h + 1]
            coef = beta * inv
            k0, k1 = k[h][:half], k[h][half:]
            n00.append(split(jnp.where(strict, coef[:half] * dot_nt(k0, k0), 0.0)))
            n11.append(split(jnp.where(strict, coef[half:] * dot_nt(k1, k1), 0.0)))
            n10.append(split(coef[half:] * dot_nt(k1, k0)))
            vf = v_all[:, span_of[h]].astype(F32) * (beta * jnp.sqrt(inv))
            rhs.append(jnp.concatenate([vf, kf * coef], axis=1))
        inverse = unit_lower_inverses([n[0] for n in n00] + [n[0] for n in n11], masks)

        def solve(t, n, r):
            zh = dot(t, r.astype(BF16)).astype(BF16)
            res = (r - zh.astype(F32)) - (dot(n[0], zh) + dot(n[1], zh))
            return zh, dot(t, res.astype(BF16)).astype(BF16)

        top = [solve(inverse[h], n00[h], rhs[h][:half]) for h in range(group)]
        low = []
        for h in range(group):
            th, tl = top[h]
            r = rhs[h][half:] - (dot(n10[h][0], th) + (dot(n10[h][1], th) + dot(n10[h][0], tl)))
            low.append(solve(inverse[group + h], n11[h], r))
        for h in range(group):
            head = step * group + h
            zh = jnp.concatenate([top[h][0], low[h][0]], axis=0)
            zl = jnp.concatenate([top[h][1], low[h][1]], axis=0)
            kz = dot_tn(k[h], zh) + dot_tn(k[h], zl)
            maps[head, :, :size] = eye - kz[:, size:]
            maps[head, :, size:] = kz[:, :size]
            zhi[h] = zh
            zlo[h] = zl

    def make_outs(step):
        tok = lax.broadcasted_iota(jnp.int32, (count, rows), 0)
        virt = lax.broadcasted_iota(jnp.int32, (count, rows), 1)
        seen = virt <= 2 * tok + 1
        k_all, q_all = k_ref[:, lanes(step)], q_ref[:, lanes(step)]
        for h in range(group):
            head = step * group + h
            q = q_all[:, span_of[h]]
            qf = q.astype(F32)
            rq = lax.rsqrt(jnp.sum(qf * qf, axis=-1, keepdims=True) + 1e-06)
            ph, plo = split(jnp.where(seen, dot_nt(q, k_all[:, span_of[h]]), 0.0))
            zh = zhi[h]
            pz = dot(ph, zh) + (dot(plo, zh) + dot(ph, zlo[h]))
            outs[head, :, :size] = pz[:, :size] * rq
            outs[head, :, size:] = (qf - pz[:, size:]) * rq

    def prefix(h, fwd):
        start, end = (first, last) if fwd else (last, first)

        @pl.when(start)
        def _():
            send_pre(h, fwd, maps, 0).start()
            send_pre(h, fwd, maps, 1).start()

        @pl.when(jnp.logical_not(start))
        def _():
            own_a, own_b = split(maps[h, :, :size]), maps[h, :, size:]
            send_pre(h, fwd, comp, 0).wait_recv()
            got_a = split(pre[h, :, :size])
            late, early = (own_a, got_a) if fwd else (got_a, own_a)
            comp[h, :, :size] = dot3_split(late, early)

            @pl.when(jnp.logical_not(end))
            def _():
                send_pre(h, fwd, comp, 0).start()

            send_pre(h, fwd, comp, 1).wait_recv()
            got_b = pre[h, :, size:]
            late_b, early_b = (own_b, got_b) if fwd else (got_b, own_b)
            comp[h, :, size:] = dot3_split(late, split(early_b)) + late_b

            @pl.when(jnp.logical_not(end))
            def _():
                send_pre(h, fwd, comp, 1).start()

    def advance(src, h):
        return dot3(src[h, :, :size], state[h]) + src[h, :, size:]

    def enter(h, fwd):
        end = last if fwd else first

        @pl.when(end & has_prev)
        def _():
            send_chain(h).wait_recv()

        @pl.when(end & jnp.logical_not(has_prev))
        def _():
            state[h] = jnp.zeros((size, size), F32)

        @pl.when(end & has_next)
        def _():
            after[h] = advance(comp, h)
            send_chain(h).start()

        @pl.when(jnp.logical_not(end))
        def _():
            send_relay(h, fwd).wait_recv()

        @pl.when(jnp.logical_not(first if fwd else last))
        def _():
            if not fwd:
                relay[h] = advance(maps, h)
            send_relay(h, fwd).start()

    def emit(j):
        def write(h, entry):
            full = outs[h, :, :size] + dot3(outs[h, :, size:], entry)
            scale = lax.rsqrt(jnp.mean(full * full, axis=-1, keepdims=True) + 1e-06)
            where = pl.ds(pl.multiple_of(h * size, size), size)
            mixed_ref[:, where] = (full * scale * gain_ref[:, where]).astype(BF16)

        write(2 * j + 1, state[2 * j + 1])
        write(2 * j, advance(pre, 2 * j))

    back = n_in - 1 - at
    shift = 2 * (n_in - 1) + grp // 2
    pairs = (
        (0, True, 2 * at, shift + 2 * back),
        (1, False, 2 * back, shift + 2 * at),
    )
    leave = shift + 2 * (n_in - 1)

    @pl.when(first)
    def _():
        unit = jnp.concatenate(
            [(row_h == col_h).astype(F32), jnp.zeros((size, size), F32)], axis=1)
        for j in range(n_pairs):
            pre[2 * j] = unit

    def sweep(t, _):
        part = t % pairs_at_once

        @pl.when((t < n_pairs) & (part == 0))
        def _():
            make_maps(t // pairs_at_once)

        @pl.when(t == 0)
        def _():
            pl.semaphore_wait(barrier, peers)

        for off, fwd, skew, _ in pairs:
            @pl.when((t >= skew) & (t < n_pairs + skew))
            def _():
                prefix((t - skew) * 2 + off, fwd)

        for off, fwd, _, skew in pairs:
            @pl.when((t >= skew) & (t < n_pairs + skew))
            def _():
                enter((t - skew) * 2 + off, fwd)

        @pl.when((t < n_pairs) & (part == pairs_at_once - 1))
        def _():
            make_outs(t // pairs_at_once)

        @pl.when((t >= leave) & (t < n_pairs + leave))
        def _():
            emit(t - leave)

        return 0

    lax.fori_loop(0, n_pairs + 4 * n_in + n_out // 2, sweep, 0)

    def drain(j, _):
        for fwd in (True, False):
            h = 2 * j + (0 if fwd else 1)
            start, end = (first, last) if fwd else (last, first)

            @pl.when(jnp.logical_not(end))
            def _():
                send_pre(h, fwd, comp, 0).wait_send()
                send_pre(h, fwd, comp, 1).wait_send()

            @pl.when(end & has_next)
            def _():
                send_chain(h).wait_send()

            @pl.when(jnp.logical_not(start))
            def _():
                send_relay(h, fwd).wait_send()

        return 0

    lax.fori_loop(0, heads // 2, drain, 0)


def local(queries, keys, values, beta_logit, gain):
    count, width = queries.shape
    heads = beta_logit.shape[1]
    size = width // heads
    rows = 2 * count
    steps = heads // GROUP
    half = rows // 2
    n_in, n_out = lax.axis_size("inner"), lax.axis_size("outer")
    k2 = keys.reshape(rows, width)
    v2 = values.reshape(rows, width)
    vmem = pl.BlockSpec(memory_space=pltpu.VMEM)
    sems = pltpu.SemaphoreType.DMA((heads,))
    sems2 = pltpu.SemaphoreType.DMA((heads, 2))
    wide = pltpu.VMEM((heads, size, 2 * size), F32)
    square = pltpu.VMEM((heads, size, size), F32)
    solved = pltpu.VMEM((GROUP, rows, 2 * size), BF16)
    return pl.pallas_call(
        functools.partial(layer_kernel, n_in, n_out),
        out_shape=jax.ShapeDtypeStruct((count, width), BF16),
        in_specs=[vmem] * 5,
        out_specs=vmem,
        scratch_shapes=[
            pltpu.VMEM((half.bit_length(), half, half), BF16),
            pltpu.VMEM((steps, rows, GROUP), F32),
            wide, solved, solved,
            pltpu.VMEM((heads, count, 2 * size), F32),
            wide, wide, square, square, square,
            sems2, sems2, sems, sems, sems,
        ],
        compiler_params=pltpu.CompilerParams(
            collective_id=0, has_side_effects=True, vmem_limit_bytes=48 * 1024 * 1024
        ),
    )(queries, k2, v2, beta_logit, gain.reshape(1, -1))


def solution(mesh):
    return jax.shard_map(
        local,
        mesh=mesh,
        in_specs=(
            P(("outer", "inner"), None),
            P(("outer", "inner"), None, None),
            P(("outer", "inner"), None, None),
            P(None, None, ("outer", "inner")),
            P(),
        ),
        out_specs=P(("outer", "inner"), None),
        check_vma=False,
    )
```

```python
import functools

import jax
import jax.numpy as jnp
from jax import lax
from jax.experimental import pallas as pl
from jax.experimental.pallas import tpu as pltpu
from jax.sharding import PartitionSpec as P

F32 = jnp.float32
BF16 = jnp.bfloat16
MESH = pl.DeviceIdType.MESH


def dot(a, b):
    return lax.dot_general(a, b, (((1,), (0,)), ((), ())), preferred_element_type=F32)


def dot_nt(a, b):
    return lax.dot_general(a, b, (((1,), (1,)), ((), ())), preferred_element_type=F32)


def dot_tn(a, b):
    return lax.dot_general(a, b, (((0,), (0,)), ((), ())), preferred_element_type=F32)


def split(x):
    hi = x.astype(BF16)
    return hi, (x - hi.astype(F32)).astype(BF16)


def dot3_split(a, b):
    return dot(a[0], b[0]) + (dot(a[0], b[1]) + dot(a[1], b[0]))


def dot3(a, b):
    return dot3_split(split(a), split(b))


def unit_lower_inverses(systems, masks):
    size = systems[0].shape[0]
    eye = masks[0]
    out = [eye - n * masks[1] for n in systems]
    levels = size.bit_length() - 2
    for level in range(levels):
        mask = masks[2 + level]
        mid = [dot(n * mask, t).astype(BF16) for n, t in zip(systems, out)]
        out = [t - dot(t, m).astype(BF16) for t, m in zip(out, mid)]
    return out


def level_masks(size):
    row = lax.broadcasted_iota(jnp.int32, (size, size), 0)
    col = lax.broadcasted_iota(jnp.int32, (size, size), 1)
    lower = row > col
    masks = [(row == col)]
    for level in range(size.bit_length() - 1):
        same = (row >> (level + 1)) == (col >> (level + 1))
        apart = (row >> level) != (col >> level)
        masks.append(lower & same & apart)
    return [m.astype(F32).astype(BF16) for m in masks]


def layer_kernel(
    n_in, n_out, q_ref, k_ref, v_ref, b_ref, gain_ref, mixed_ref,
    mask_ref, beta_ref, maps, zhi, zlo, outs, comp, pre, state, after, relay,
    s_pre, r_pre, s_chain, s_relay, r_state,
):
    heads, size = maps.shape[0], maps.shape[1]
    count, rows = q_ref.shape[0], k_ref.shape[0]
    half = rows // 2
    n_pairs = heads // 2
    at, grp = lax.axis_index("inner"), lax.axis_index("outer")
    first, last = at == 0, at == n_in - 1
    has_prev = grp > 0
    has_next = grp < n_out - 1
    ends = first | last

    barrier = pltpu.get_barrier_semaphore()
    greetings = (
        (at > 0, (grp, at - 1)),
        (at < n_in - 1, (grp, at + 1)),
        (ends & has_prev, (grp - 1, at)),
        (ends & has_next, (grp + 1, at)),
    )
    for cond, dev in greetings:
        @pl.when(cond)
        def _():
            pl.semaphore_signal(barrier, inc=1, device_id=dev, device_id_type=MESH)

    for where, m in enumerate(level_masks(half)):
        mask_ref[where] = m
    spot = lax.broadcasted_iota(jnp.int32, (rows, count), 0)
    token = lax.broadcasted_iota(jnp.int32, (rows, count), 1)
    spread = jnp.zeros((rows, heads), F32)
    for j in range(2):
        pick = (spot == 2 * token + j).astype(F32).astype(BF16)
        strength = 2.0 / (1.0 + jnp.exp(-b_ref[j]))
        for _ in range(3):
            part = strength.astype(BF16)
            strength = strength - part.astype(F32)
            spread = spread + dot_nt(pick, part)
    for j in range(n_pairs):
        beta_ref[j] = spread[:, 2 * j : 2 * j + 2]
    peers = sum(c.astype(jnp.int32) for c, _ in greetings)

    parts = (slice(0, size), slice(size, 2 * size))

    def send_pre(h, fwd, src, piece):
        return pltpu.make_async_remote_copy(
            src.at[h, :, parts[piece]], pre.at[h, :, parts[piece]],
            s_pre.at[h, piece], r_pre.at[h, piece],
            device_id=(grp, at + 1 if fwd else at - 1), device_id_type=MESH)

    def send_chain(h):
        return pltpu.make_async_remote_copy(
            after.at[h], state.at[h], s_chain.at[h], r_state.at[h],
            device_id=(grp + 1, at), device_id_type=MESH)

    def send_relay(h, fwd):
        src = state if fwd else relay
        return pltpu.make_async_remote_copy(
            src.at[h], state.at[h], s_relay.at[h], r_state.at[h],
            device_id=(grp, at - 1 if fwd else at + 1), device_id_type=MESH)

    row_h = lax.broadcasted_iota(jnp.int32, (half, half), 0)
    col_h = lax.broadcasted_iota(jnp.int32, (half, half), 1)

    def lanes(pair, group):
        return pl.ds(pl.multiple_of(pair * 2 * size, 2 * size), group * size)

    def make_maps(pair, group):
        span_of = [slice(h * size, (h + 1) * size) for h in range(group)]
        masks = [mask_ref[m] for m in range(mask_ref.shape[0])]
        strict = row_h > col_h
        eye = (row_h == col_h).astype(F32)
        beta_pairs = [beta_ref[pair + j] for j in range(group // 2)]
        k_all, v_all = k_ref[:, lanes(pair, group)], v_ref[:, lanes(pair, group)]
        k = [k_all[:, c] for c in span_of]
        n00, n10, n11, rhs = [], [], [], []
        for h in range(group):
            kf = k[h].astype(F32)
            inv = 1.0 / (jnp.sum(kf * kf, axis=-1, keepdims=True) + 1e-06)
            beta = beta_pairs[h // 2][:, h % 2 : h % 2 + 1]
            coef = beta * inv
            k0, k1 = k[h][:half], k[h][half:]
            n00.append(split(jnp.where(strict, coef[:half] * dot_nt(k0, k0), 0.0)))
            n11.append(split(jnp.where(strict, coef[half:] * dot_nt(k1, k1), 0.0)))
            n10.append(split(coef[half:] * dot_nt(k1, k0)))
            vf = v_all[:, span_of[h]].astype(F32) * (beta * jnp.sqrt(inv))
            rhs.append(jnp.concatenate([vf, kf * coef], axis=1))
        inverse = unit_lower_inverses([n[0] for n in n00] + [n[0] for n in n11], masks)

        def solve(t, n, r):
            zh = dot(t, r.astype(BF16)).astype(BF16)
            res = (r - zh.astype(F32)) - (dot(n[0], zh) + dot(n[1], zh))
            return zh, dot(t, res.astype(BF16)).astype(BF16)

        top = [solve(inverse[h], n00[h], rhs[h][:half]) for h in range(group)]
        low = []
        for h in range(group):
            th, tl = top[h]
            r = rhs[h][half:] - (dot(n10[h][0], th) + (dot(n10[h][1], th) + dot(n10[h][0], tl)))
            low.append(solve(inverse[group + h], n11[h], r))
        for h in range(group):
            head = 2 * pair + h
            zh = jnp.concatenate([top[h][0], low[h][0]], axis=0)
            zl = jnp.concatenate([top[h][1], low[h][1]], axis=0)
            kz = dot_tn(k[h], zh) + dot_tn(k[h], zl)
            maps[head, :, :size] = eye - kz[:, size:]
            maps[head, :, size:] = kz[:, :size]
            zhi[head] = zh
            zlo[head] = zl

    def make_outs(pair, group):
        span_of = [slice(h * size, (h + 1) * size) for h in range(group)]
        tok = lax.broadcasted_iota(jnp.int32, (count, rows), 0)
        virt = lax.broadcasted_iota(jnp.int32, (count, rows), 1)
        seen = virt <= 2 * tok + 1
        k_all, q_all = k_ref[:, lanes(pair, group)], q_ref[:, lanes(pair, group)]
        for h in range(group):
            head = 2 * pair + h
            q = q_all[:, span_of[h]]
            qf = q.astype(F32)
            rq = lax.rsqrt(jnp.sum(qf * qf, axis=-1, keepdims=True) + 1e-06)
            ph, plo = split(jnp.where(seen, dot_nt(q, k_all[:, span_of[h]]), 0.0))
            zh = zhi[head]
            pz = dot(ph, zh) + (dot(plo, zh) + dot(ph, zlo[head]))
            outs[head, :, :size] = pz[:, :size] * rq
            outs[head, :, size:] = (qf - pz[:, size:]) * rq

    def prefix(h, fwd):
        start, end = (first, last) if fwd else (last, first)

        @pl.when(start)
        def _():
            send_pre(h, fwd, maps, 0).start()
            send_pre(h, fwd, maps, 1).start()

        @pl.when(jnp.logical_not(start))
        def _():
            own_a, own_b = split(maps[h, :, :size]), maps[h, :, size:]
            send_pre(h, fwd, comp, 0).wait_recv()
            got_a = split(pre[h, :, :size])
            late, early = (own_a, got_a) if fwd else (got_a, own_a)
            comp[h, :, :size] = dot3_split(late, early)

            @pl.when(jnp.logical_not(end))
            def _():
                send_pre(h, fwd, comp, 0).start()

            send_pre(h, fwd, comp, 1).wait_recv()
            got_b = pre[h, :, size:]
            late_b, early_b = (own_b, got_b) if fwd else (got_b, own_b)
            comp[h, :, size:] = dot3_split(late, split(early_b)) + late_b

            @pl.when(jnp.logical_not(end))
            def _():
                send_pre(h, fwd, comp, 1).start()

    def advance(src, h):
        return dot3(src[h, :, :size], state[h]) + src[h, :, size:]

    def enter(h, fwd):
        end = last if fwd else first

        @pl.when(end & has_prev)
        def _():
            send_chain(h).wait_recv()

        @pl.when(end & jnp.logical_not(has_prev))
        def _():
            state[h] = jnp.zeros((size, size), F32)

        @pl.when(end & has_next)
        def _():
            after[h] = advance(comp, h)
            send_chain(h).start()

        @pl.when(jnp.logical_not(end))
        def _():
            send_relay(h, fwd).wait_recv()

        @pl.when(jnp.logical_not(first if fwd else last))
        def _():
            if not fwd:
                relay[h] = advance(maps, h)
            send_relay(h, fwd).start()

    def emit(j):
        def write(h, entry):
            full = outs[h, :, :size] + dot3(outs[h, :, size:], entry)
            scale = lax.rsqrt(jnp.mean(full * full, axis=-1, keepdims=True) + 1e-06)
            where = pl.ds(pl.multiple_of(h * size, size), size)
            mixed_ref[:, where] = (full * scale * gain_ref[:, where]).astype(BF16)

        write(2 * j + 1, state[2 * j + 1])
        write(2 * j, advance(pre, 2 * j))

    back = n_in - 1 - at
    shift = 2 * (n_in - 1) + grp // 2
    pairs = (
        (0, True, 2 * at, shift + 2 * back),
        (1, False, 2 * back, shift + 2 * at),
    )
    leave = shift + 2 * (n_in - 1)

    @pl.when(first)
    def _():
        unit = jnp.concatenate(
            [(row_h == col_h).astype(F32), jnp.zeros((size, size), F32)], axis=1)
        for j in range(n_pairs):
            pre[2 * j] = unit

    def sweep(t, _):
        @pl.when(t < 2)
        def _():
            make_maps(t, 2)

        @pl.when((t % 2 == 0) & (t >= 2) & (t < n_pairs))
        def _():
            make_maps(t, 4)

        @pl.when(t == 0)
        def _():
            pl.semaphore_wait(barrier, peers)

        for off, fwd, skew, _ in pairs:
            @pl.when((t >= skew) & (t < n_pairs + skew))
            def _():
                prefix((t - skew) * 2 + off, fwd)

        for off, fwd, _, skew in pairs:
            @pl.when((t >= skew) & (t < n_pairs + skew))
            def _():
                enter((t - skew) * 2 + off, fwd)

        @pl.when((t % 2 == 1) & (t < n_pairs))
        def _():
            make_outs(t - 1, 4)

        @pl.when((t >= leave) & (t < n_pairs + leave))
        def _():
            emit(t - leave)

        return 0

    lax.fori_loop(0, n_pairs + 4 * n_in + n_out // 2, sweep, 0)

    def drain(j, _):
        for fwd in (True, False):
            h = 2 * j + (0 if fwd else 1)
            start, end = (first, last) if fwd else (last, first)

            @pl.when(jnp.logical_not(end))
            def _():
                send_pre(h, fwd, comp, 0).wait_send()
                send_pre(h, fwd, comp, 1).wait_send()

            @pl.when(end & has_next)
            def _():
                send_chain(h).wait_send()

            @pl.when(jnp.logical_not(start))
            def _():
                send_relay(h, fwd).wait_send()

        return 0

    lax.fori_loop(0, heads // 2, drain, 0)


def local(queries, keys, values, beta_logit, gain):
    count, width = queries.shape
    heads = beta_logit.shape[1]
    size = width // heads
    rows = 2 * count
    half = rows // 2
    n_in, n_out = lax.axis_size("inner"), lax.axis_size("outer")
    k2 = keys.reshape(rows, width)
    v2 = values.reshape(rows, width)
    vmem = pl.BlockSpec(memory_space=pltpu.VMEM)
    sems = pltpu.SemaphoreType.DMA((heads,))
    sems2 = pltpu.SemaphoreType.DMA((heads, 2))
    wide = pltpu.VMEM((heads, size, 2 * size), F32)
    square = pltpu.VMEM((heads, size, size), F32)
    solved = pltpu.VMEM((heads, rows, 2 * size), BF16)
    return pl.pallas_call(
        functools.partial(layer_kernel, n_in, n_out),
        out_shape=jax.ShapeDtypeStruct((count, width), BF16),
        in_specs=[vmem] * 5,
        out_specs=vmem,
        scratch_shapes=[
            pltpu.VMEM((half.bit_length(), half, half), BF16),
            pltpu.VMEM((heads // 2, rows, 2), F32),
            wide, solved, solved,
            pltpu.VMEM((heads, count, 2 * size), F32),
            wide, wide, square, square, square,
            sems2, sems2, sems, sems, sems,
        ],
        compiler_params=pltpu.CompilerParams(
            collective_id=0, has_side_effects=True, vmem_limit_bytes=48 * 1024 * 1024
        ),
    )(queries, k2, v2, beta_logit, gain.reshape(1, -1))


def solution(mesh):
    return jax.shard_map(
        local,
        mesh=mesh,
        in_specs=(
            P(("outer", "inner"), None),
            P(("outer", "inner"), None, None),
            P(("outer", "inner"), None, None),
            P(None, None, ("outer", "inner")),
            P(),
        ),
        out_specs=P(("outer", "inner"), None),
        check_vma=False,
    )
```

```python
import functools

import jax
import jax.numpy as jnp
from jax import lax
from jax.experimental import pallas as pl
from jax.experimental.pallas import tpu as pltpu
from jax.sharding import PartitionSpec as P

F32 = jnp.float32
BF16 = jnp.bfloat16
MESH = pl.DeviceIdType.MESH
GROUP = 4


def dot(a, b):
    return lax.dot_general(a, b, (((1,), (0,)), ((), ())), preferred_element_type=F32)


def dot_nt(a, b):
    return lax.dot_general(a, b, (((1,), (1,)), ((), ())), preferred_element_type=F32)


def dot_tn(a, b):
    return lax.dot_general(a, b, (((0,), (0,)), ((), ())), preferred_element_type=F32)


def split(x):
    hi = x.astype(BF16)
    return hi, (x - hi.astype(F32)).astype(BF16)


def dot3_split(a, b):
    return dot(a[0], b[0]) + (dot(a[0], b[1]) + dot(a[1], b[0]))


def dot3(a, b):
    return dot3_split(split(a), split(b))


def unit_lower_inverses(systems, masks):
    size = systems[0].shape[0]
    eye = masks[0]
    out = [eye - n * masks[1] for n in systems]
    levels = size.bit_length() - 2
    for level in range(levels):
        mask = masks[2 + level]
        mid = [dot(n * mask, t).astype(BF16) for n, t in zip(systems, out)]
        out = [t - dot(t, m).astype(BF16) for t, m in zip(out, mid)]
    return out


def level_masks(size):
    row = lax.broadcasted_iota(jnp.int32, (size, size), 0)
    col = lax.broadcasted_iota(jnp.int32, (size, size), 1)
    lower = row > col
    masks = [(row == col)]
    for level in range(size.bit_length() - 1):
        same = (row >> (level + 1)) == (col >> (level + 1))
        apart = (row >> level) != (col >> level)
        masks.append(lower & same & apart)
    return [m.astype(F32).astype(BF16) for m in masks]


def layer_kernel(
    n_in, n_out, q_ref, k_ref, v_ref, b_ref, gain_ref, mixed_ref,
    mask_ref, beta_ref, maps, zhi, zlo, outs, comp, pre, state, after, relay,
    s_pre, r_pre, s_chain, s_relay, r_state,
):
    heads, size = maps.shape[0], maps.shape[1]
    count, rows = q_ref.shape[0], k_ref.shape[0]
    half = rows // 2
    steps, group = beta_ref.shape[0], beta_ref.shape[2]
    n_pairs, pairs_at_once = heads // 2, group // 2
    span = group * size
    at, grp = lax.axis_index("inner"), lax.axis_index("outer")
    first, last = at == 0, at == n_in - 1
    has_prev = grp > 0
    has_next = grp < n_out - 1
    ends = first | last

    barrier = pltpu.get_barrier_semaphore()
    greetings = (
        (at > 0, (grp, at - 1)),
        (at < n_in - 1, (grp, at + 1)),
        (ends & has_prev, (grp - 1, at)),
        (ends & has_next, (grp + 1, at)),
    )
    for cond, dev in greetings:
        @pl.when(cond)
        def _():
            pl.semaphore_signal(barrier, inc=1, device_id=dev, device_id_type=MESH)

    for where, m in enumerate(level_masks(half)):
        mask_ref[where] = m
    spot = lax.broadcasted_iota(jnp.int32, (rows, count), 0)
    token = lax.broadcasted_iota(jnp.int32, (rows, count), 1)
    spread = jnp.zeros((rows, heads), F32)
    for j in range(2):
        pick = (spot == 2 * token + j).astype(F32).astype(BF16)
        strength = 2.0 / (1.0 + jnp.exp(-b_ref[j]))
        for _ in range(3):
            part = strength.astype(BF16)
            strength = strength - part.astype(F32)
            spread = spread + dot_nt(pick, part)
    for step in range(steps):
        beta_ref[step] = spread[:, step * group : (step + 1) * group]
    peers = sum(c.astype(jnp.int32) for c, _ in greetings)

    parts = (slice(0, size), slice(size, 2 * size))

    def send_pre(h, fwd, src, piece):
        return pltpu.make_async_remote_copy(
            src.at[h, :, parts[piece]], pre.at[h, :, parts[piece]],
            s_pre.at[h, piece], r_pre.at[h, piece],
            device_id=(grp, at + 1 if fwd else at - 1), device_id_type=MESH)

    def send_chain(h):
        return pltpu.make_async_remote_copy(
            after.at[h], state.at[h], s_chain.at[h], r_state.at[h],
            device_id=(grp + 1, at), device_id_type=MESH)

    def send_relay(h, fwd):
        src = state if fwd else relay
        return pltpu.make_async_remote_copy(
            src.at[h], state.at[h], s_relay.at[h], r_state.at[h],
            device_id=(grp, at - 1 if fwd else at + 1), device_id_type=MESH)

    row_h = lax.broadcasted_iota(jnp.int32, (half, half), 0)
    col_h = lax.broadcasted_iota(jnp.int32, (half, half), 1)
    span_of = [slice(h * size, (h + 1) * size) for h in range(group)]

    def lanes(step):
        return pl.ds(pl.multiple_of(step * span, span), span)

    def make_maps(step):
        masks = [mask_ref[m] for m in range(mask_ref.shape[0])]
        strict = row_h > col_h
        eye = (row_h == col_h).astype(F32)
        beta_all = beta_ref[step]
        k_all, v_all = k_ref[:, lanes(step)], v_ref[:, lanes(step)]
        k = [k_all[:, c] for c in span_of]
        n00, n10, n11, rhs = [], [], [], []
        for h in range(group):
            kf = k[h].astype(F32)
            inv = 1.0 / (jnp.sum(kf * kf, axis=-1, keepdims=True) + 1e-06)
            beta = beta_all[:, h : h + 1]
            coef = beta * inv
            k0, k1 = k[h][:half], k[h][half:]
            n00.append(split(jnp.where(strict, coef[:half] * dot_nt(k0, k0), 0.0)))
            n11.append(split(jnp.where(strict, coef[half:] * dot_nt(k1, k1), 0.0)))
            n10.append(split(coef[half:] * dot_nt(k1, k0)))
            vf = v_all[:, span_of[h]].astype(F32) * (beta * jnp.sqrt(inv))
            rhs.append(jnp.concatenate([vf, kf * coef], axis=1))
        inverse = unit_lower_inverses([n[0] for n in n00] + [n[0] for n in n11], masks)

        def solve(t, n, r):
            zh = dot(t, r.astype(BF16)).astype(BF16)
            res = (r - zh.astype(F32)) - (dot(n[0], zh) + dot(n[1], zh))
            return zh, dot(t, res.astype(BF16)).astype(BF16)

        top = [solve(inverse[h], n00[h], rhs[h][:half]) for h in range(group)]
        low = []
        for h in range(group):
            th, tl = top[h]
            r = rhs[h][half:] - (dot(n10[h][0], th) + (dot(n10[h][1], th) + dot(n10[h][0], tl)))
            low.append(solve(inverse[group + h], n11[h], r))
        for h in range(group):
            head = step * group + h
            zh = jnp.concatenate([top[h][0], low[h][0]], axis=0)
            zl = jnp.concatenate([top[h][1], low[h][1]], axis=0)
            kz = dot_tn(k[h], zh) + dot_tn(k[h], zl)
            maps[head, :, :size] = eye - kz[:, size:]
            maps[head, :, size:] = kz[:, :size]
            zhi[head] = zh
            zlo[head] = zl

    def make_outs(step):
        tok = lax.broadcasted_iota(jnp.int32, (count, rows), 0)
        virt = lax.broadcasted_iota(jnp.int32, (count, rows), 1)
        seen = virt <= 2 * tok + 1
        k_all, q_all = k_ref[:, lanes(step)], q_ref[:, lanes(step)]
        for h in range(group):
            head = step * group + h
            q = q_all[:, span_of[h]]
            qf = q.astype(F32)
            rq = lax.rsqrt(jnp.sum(qf * qf, axis=-1, keepdims=True) + 1e-06)
            ph, plo = split(jnp.where(seen, dot_nt(q, k_all[:, span_of[h]]), 0.0))
            zh = zhi[head]
            pz = dot(ph, zh) + (dot(plo, zh) + dot(ph, zlo[head]))
            outs[head, :, :size] = pz[:, :size] * rq
            outs[head, :, size:] = (qf - pz[:, size:]) * rq

    def prefix(h, fwd):
        start, end = (first, last) if fwd else (last, first)

        @pl.when(start)
        def _():
            send_pre(h, fwd, maps, 0).start()
            send_pre(h, fwd, maps, 1).start()

        @pl.when(jnp.logical_not(start))
        def _():
            own_a, own_b = split(maps[h, :, :size]), maps[h, :, size:]
            send_pre(h, fwd, comp, 0).wait_recv()
            got_a = split(pre[h, :, :size])
            late, early = (own_a, got_a) if fwd else (got_a, own_a)
            comp[h, :, :size] = dot3_split(late, early)

            @pl.when(jnp.logical_not(end))
            def _():
                send_pre(h, fwd, comp, 0).start()

            send_pre(h, fwd, comp, 1).wait_recv()
            got_b = pre[h, :, size:]
            late_b, early_b = (own_b, got_b) if fwd else (got_b, own_b)
            comp[h, :, size:] = dot3_split(late, split(early_b)) + late_b

            @pl.when(jnp.logical_not(end))
            def _():
                send_pre(h, fwd, comp, 1).start()

    def advance(src, h):
        return dot3(src[h, :, :size], state[h]) + src[h, :, size:]

    def enter(h, fwd):
        end = last if fwd else first

        @pl.when(end & has_prev)
        def _():
            send_chain(h).wait_recv()

        @pl.when(end & jnp.logical_not(has_prev))
        def _():
            state[h] = jnp.zeros((size, size), F32)

        @pl.when(end & has_next)
        def _():
            after[h] = advance(comp, h)
            send_chain(h).start()

        @pl.when(jnp.logical_not(end))
        def _():
            send_relay(h, fwd).wait_recv()

        @pl.when(jnp.logical_not(first if fwd else last))
        def _():
            if not fwd:
                relay[h] = advance(maps, h)
            send_relay(h, fwd).start()

    def emit(j):
        def write(h, entry):
            full = outs[h, :, :size] + dot3(outs[h, :, size:], entry)
            scale = lax.rsqrt(jnp.mean(full * full, axis=-1, keepdims=True) + 1e-06)
            where = pl.ds(pl.multiple_of(h * size, size), size)
            mixed_ref[:, where] = (full * scale * gain_ref[:, where]).astype(BF16)

        write(2 * j + 1, state[2 * j + 1])
        write(2 * j, advance(pre, 2 * j))

    back = n_in - 1 - at
    shift = 2 * (n_in - 1) + grp // 2
    pairs = (
        (0, True, 2 * at, shift + 2 * back),
        (1, False, 2 * back, shift + 2 * at),
    )
    leave = shift + 2 * (n_in - 1)

    @pl.when(first)
    def _():
        unit = jnp.concatenate(
            [(row_h == col_h).astype(F32), jnp.zeros((size, size), F32)], axis=1)
        for j in range(n_pairs):
            pre[2 * j] = unit

    def sweep(t, _):
        part = t % pairs_at_once

        @pl.when((t < n_pairs) & (part == 0))
        def _():
            make_maps(t // pairs_at_once)

        @pl.when(t == 0)
        def _():
            pl.semaphore_wait(barrier, peers)

        for off, fwd, skew, _ in pairs:
            @pl.when((t >= skew) & (t < n_pairs + skew))
            def _():
                prefix((t - skew) * 2 + off, fwd)

        for off, fwd, _, skew in pairs:
            @pl.when((t >= skew) & (t < n_pairs + skew))
            def _():
                enter((t - skew) * 2 + off, fwd)

        @pl.when((t >= n_pairs) & (t < n_pairs + steps))
        def _():
            make_outs(t - n_pairs)

        @pl.when((t >= leave) & (t < n_pairs + leave))
        def _():
            emit(t - leave)

        return 0

    lax.fori_loop(0, n_pairs + 4 * n_in + n_out // 2, sweep, 0)

    def drain(j, _):
        for fwd in (True, False):
            h = 2 * j + (0 if fwd else 1)
            start, end = (first, last) if fwd else (last, first)

            @pl.when(jnp.logical_not(end))
            def _():
                send_pre(h, fwd, comp, 0).wait_send()
                send_pre(h, fwd, comp, 1).wait_send()

            @pl.when(end & has_next)
            def _():
                send_chain(h).wait_send()

            @pl.when(jnp.logical_not(start))
            def _():
                send_relay(h, fwd).wait_send()

        return 0

    lax.fori_loop(0, heads // 2, drain, 0)


def local(queries, keys, values, beta_logit, gain):
    count, width = queries.shape
    heads = beta_logit.shape[1]
    size = width // heads
    rows = 2 * count
    steps = heads // GROUP
    half = rows // 2
    n_in, n_out = lax.axis_size("inner"), lax.axis_size("outer")
    k2 = keys.reshape(rows, width)
    v2 = values.reshape(rows, width)
    vmem = pl.BlockSpec(memory_space=pltpu.VMEM)
    sems = pltpu.SemaphoreType.DMA((heads,))
    sems2 = pltpu.SemaphoreType.DMA((heads, 2))
    wide = pltpu.VMEM((heads, size, 2 * size), F32)
    square = pltpu.VMEM((heads, size, size), F32)
    solved = pltpu.VMEM((heads, rows, 2 * size), BF16)
    return pl.pallas_call(
        functools.partial(layer_kernel, n_in, n_out),
        out_shape=jax.ShapeDtypeStruct((count, width), BF16),
        in_specs=[vmem] * 5,
        out_specs=vmem,
        scratch_shapes=[
            pltpu.VMEM((half.bit_length(), half, half), BF16),
            pltpu.VMEM((steps, rows, GROUP), F32),
            wide, solved, solved,
            pltpu.VMEM((heads, count, 2 * size), F32),
            wide, wide, square, square, square,
            sems2, sems2, sems, sems, sems,
        ],
        compiler_params=pltpu.CompilerParams(
            collective_id=0, has_side_effects=True, vmem_limit_bytes=48 * 1024 * 1024
        ),
    )(queries, k2, v2, beta_logit, gain.reshape(1, -1))


def solution(mesh):
    return jax.shard_map(
        local,
        mesh=mesh,
        in_specs=(
            P(("outer", "inner"), None),
            P(("outer", "inner"), None, None),
            P(("outer", "inner"), None, None),
            P(None, None, ("outer", "inner")),
            P(),
        ),
        out_specs=P(("outer", "inner"), None),
        check_vma=False,
    )
```
